32 devices in a mesh: group: 2 (over x), gx: 8 (over z, y), gy: 2 (over core).
Axes of the slice: x: 2, y: 2, z: 4, core: 2. Of those that a mesh axis runs over, the one named last changes fastest.
Arguments:
- easting_current: float32 [16, 1024, 256], P(None, ('group', 'gx'), 'gy'), parts along dimension 1, may hold values from -3 to 3
- poleward_current: float32 [16, 1024, 256], P(None, ('group', 'gx'), 'gy'), parts along dimension 1, may hold values from -3 to 3
- thermal_anomaly: float32 [16, 1024, 256], P(None, ('group', 'gx'), 'gy'), parts along dimension 1, may hold values from -6 to 6
- planetary_spin_parameter: float32 [512], P('gx'), may hold values from -1 to 1
- stratum_spacings: float32 [16], replicated, may hold values from 0.5 to 2
- sideways_diffusivity: float32 [512, 256], P('gx', 'gy'), may hold values from 0.03 to 0.2
- bathymetry_multiplier: float32 [512, 256], P('gx', 'gy'), may hold values from 0.5 to 2
- sea_level_elevation: float32 [1024, 256], P(('group', 'gx'), 'gy'), parts along dimension 0, may hold values from -12 to 12
- wet_dry_indicator: int32 [8, 4], replicated, may hold values 0 or 1
Outputs:
- easting_current_next: float32 [16, 1024, 256], P(None, ('group', 'gx'), 'gy'), parts along dimension 1
- poleward_current_next: float32 [16, 1024, 256], P(None, ('group', 'gx'), 'gy'), parts along dimension 1
- thermal_anomaly_next: float32 [16, 1024, 256], P(None, ('group', 'gx'), 'gy'), parts along dimension 1
- barotropic_guess: float32 [1024, 256], P(('group', 'gx'), 'gy'), parts along dimension 0
- equation_misfit: float32 [1024, 256], P(('group', 'gx'), 'gy'), parts along dimension 0
The draws below stay inside these ranges and needn't reach their ends.
There are 2 independent parts, one for each index of `group`. The reference program is written for one: setup_inputs(seed, part) draws one part's arguments, and reference() takes and returns one part's arrays. A program takes and returns all parts, laid end to end along the dimension named above; an argument that names none is the same for every part. Nothing has to cross between parts.
All inputs are finite; a program needn't handle non-finite values.
Results may differ from the reference program's by a relative error of at most 0.0003.
Values sent between devices are 32-bit elements; how exact they have to be, the bound alone decides.
A program may use at most 128 MiB of HBM per device.

```python
import math
import jax
import jax.numpy as jnp
from jax import lax

VERTICAL_STRATA = 16
TS = 64
ITERS = 3
MESH_Y_EXTENT = 512
MESH_X_EXTENT = 256
NTX = 8
NTY = 4


def draw_sea_level_elevation(key, part):
    key = jax.random.fold_in(key, 11)
    positions = jnp.arange(MESH_Y_EXTENT, dtype=jnp.float32) / max(MESH_Y_EXTENT - 1, 1)
    ramp = (1.0 + 2.0 * positions)[:, None]
    return jnp.clip(jax.random.normal(key, (MESH_Y_EXTENT, MESH_X_EXTENT), jnp.float32), -4.0, 4.0) * ramp


def touch_ends(array, own_key, low, largest):
    longest = array.shape.index(max(array.shape))
    spots = []
    for shift in (0, 1):
        where = [jax.random.randint(jax.random.fold_in(own_key, axis), (), 0, length) for axis, length in enumerate(array.shape)]
        where[longest] = (where[longest] + shift) % array.shape[longest]
        spots.append(tuple(where))
    return array.at[spots[0]].set(low).at[spots[1]].set(largest)


def steps_of(stream_key, extent, shards, low, top_value):
    def one(axis_at, blocks):
        steps = jax.random.uniform(jax.random.fold_in(jax.random.fold_in(stream_key, 6), axis_at), (blocks,), jnp.float32, low / len(shards), top_value / len(shards))
        return jnp.repeat(jnp.exp(steps), extent[axis_at] // blocks).reshape((-1,) + (1,) * (len(extent) - axis_at - 1))

    factor_of = one(*shards[0])
    for cut in shards[1:]:
        factor_of = factor_of * one(*cut)
    return factor_of


def centred(own_key, dims, scale, most, shards=(), held_as=jnp.bfloat16):
    entries = scale * jax.random.normal(own_key, dims, jnp.float32)
    if shards:
        entries = entries * steps_of(own_key, dims, shards, -0.22, 0.18)
    return jnp.clip(entries, -most, most).astype(held_as)


def setup_inputs(seed: int = 0, part: int = 0) -> dict:
    seeds = jax.random.split(jax.random.key(seed), 10)
    own_keys = jax.random.split(jax.random.fold_in(seeds[9], part), 10)
    return {
        "easting_current": centred(own_keys[0], (VERTICAL_STRATA, MESH_Y_EXTENT, MESH_X_EXTENT), 0.5, 3.0, ((1, 8), (2, 2)), jnp.float32),
        "poleward_current": centred(own_keys[1], (VERTICAL_STRATA, MESH_Y_EXTENT, MESH_X_EXTENT), 0.5, 3.0, ((1, 8), (2, 2)), jnp.float32),
        "thermal_anomaly": centred(own_keys[2], (VERTICAL_STRATA, MESH_Y_EXTENT, MESH_X_EXTENT), 1.0, 6.0, ((1, 8), (2, 2)), jnp.float32),
        "planetary_spin_parameter": jnp.clip(jax.random.uniform(seeds[3], (MESH_Y_EXTENT,), jnp.float32, -1.0, 1.0) * steps_of(seeds[3], (MESH_Y_EXTENT,), ((0, 8),), -0.4, 0.0), -1.0, 1.0),
        "stratum_spacings": jnp.clip(jnp.exp(jax.random.uniform(seeds[4], (VERTICAL_STRATA,), jnp.float32, math.log(0.5), math.log(2.0))), 0.5, 2.0),
        "sideways_diffusivity": jnp.clip(jnp.exp(math.log(0.2) - 1.89712 * jax.random.uniform(seeds[5], (MESH_Y_EXTENT, MESH_X_EXTENT), jnp.float32) ** steps_of(seeds[5], (MESH_Y_EXTENT, MESH_X_EXTENT), ((0, 8), (1, 2)), -0.2, 0.2)), 0.03, 0.2),
        "bathymetry_multiplier": jnp.clip(jnp.exp(math.log(2.0) - 1.3862944 * jax.random.uniform(seeds[6], (MESH_Y_EXTENT, MESH_X_EXTENT), jnp.float32) ** steps_of(seeds[6], (MESH_Y_EXTENT, MESH_X_EXTENT), ((0, 8), (1, 2)), -0.2, 0.2)), 0.5, 2.0),
        "sea_level_elevation": draw_sea_level_elevation(jax.random.fold_in(jax.random.fold_in(seeds[9], part), 71), part),
        "wet_dry_indicator": touch_ends((jax.random.randint(seeds[8], (NTX, NTY), 0, 4) < 3).astype(jnp.int32), jax.random.fold_in(seeds[8], 1), 0, 1),
    }


pressure_coef = 0.02
biharmonic_coef = 0.02
advection_coef = 0.5
surface_coef = 0.5
divergence_coef = 0.1


def ocean_cells(wet_dry_indicator, row_start, column_start, row_count, column_count, margin):
    tile_rows = wet_dry_indicator.shape[0]
    tile_columns = wet_dry_indicator.shape[1]
    row_index = row_start - margin + jnp.arange(row_count + 2 * margin, dtype=jnp.int32)
    column_index = column_start - margin + jnp.arange(column_count + 2 * margin, dtype=jnp.int32)
    row_pick = ((row_index[:, None] // TS == jnp.arange(tile_rows, dtype=jnp.int32)[None, :]) & (row_index[:, None] >= 0)).astype(jnp.float32)
    column_pick = ((column_index[:, None] // TS == jnp.arange(tile_columns, dtype=jnp.int32)[None, :]) & (column_index[:, None] >= 0)).astype(jnp.float32)
    tiles = wet_dry_indicator.astype(jnp.float32)
    partial_rows = jnp.dot(row_pick, tiles, precision=lax.Precision.HIGHEST)
    return jnp.dot(partial_rows, column_pick.T, precision=lax.Precision.HIGHEST)


def faces(wet_cell_indicator, coefficient):
    row_faces = 0.5 * (coefficient[1:, :] + coefficient[:-1, :]) * wet_cell_indicator[1:, :] * wet_cell_indicator[:-1, :]
    column_faces = 0.5 * (coefficient[:, 1:] + coefficient[:, :-1]) * wet_cell_indicator[:, 1:] * wet_cell_indicator[:, :-1]
    return row_faces, column_faces


def diffuse(values, row_faces, column_faces):
    flux_row = row_faces * (values[..., 1:, :] - values[..., :-1, :])
    flux_column = column_faces * (values[..., :, 1:] - values[..., :, :-1])
    return (flux_row[..., 1:, 1:-1] - flux_row[..., :-1, 1:-1]) + (flux_column[..., 1:-1, 1:] - flux_column[..., 1:-1, :-1])


def stratified_advance(haloed_array, wet_cell_indicator, planetary_spin_parameter, stratum_spacings):
    levels = stratum_spacings.shape[0]
    zonal = haloed_array[:levels]
    meridional = haloed_array[levels:2 * levels]
    tracer = haloed_array[2 * levels:3 * levels]
    viscosity = haloed_array[3 * levels]
    unit_rows, unit_columns = faces(wet_cell_indicator, jnp.ones_like(wet_cell_indicator))
    inner_rows = unit_rows[1:-1, 1:-1]
    inner_columns = unit_columns[1:-1, 1:-1]
    mask_inner = wet_cell_indicator[1:-1, 1:-1]
    visc_rows, visc_columns = faces(mask_inner, viscosity[1:-1, 1:-1])
    zonal_inner = zonal[:, 1:-1, 1:-1]
    meridional_inner = meridional[:, 1:-1, 1:-1]
    tracer_inner = tracer[:, 1:-1, 1:-1]
    thickness = stratum_spacings[:, None, None]
    column = tracer_inner * thickness
    geopotential = jnp.cumsum(column, axis=0) - 0.5 * column
    centre = geopotential[:, 1:-1, 1:-1]
    grad_row = 0.5 * (mask_inner[2:, 1:-1] * (geopotential[:, 2:, 1:-1] - centre) + mask_inner[:-2, 1:-1] * (centre - geopotential[:, :-2, 1:-1]))
    grad_column = 0.5 * (mask_inner[1:-1, 2:] * (geopotential[:, 1:-1, 2:] - centre) + mask_inner[1:-1, :-2] * (centre - geopotential[:, 1:-1, :-2]))
    flux_row = 0.25 * (zonal_inner[:, 1:, :] + zonal_inner[:, :-1, :]) * (tracer_inner[:, 1:, :] + tracer_inner[:, :-1, :]) * inner_rows
    flux_column = 0.25 * (meridional_inner[:, :, 1:] + meridional_inner[:, :, :-1]) * (tracer_inner[:, :, 1:] + tracer_inner[:, :, :-1]) * inner_columns
    spread = (flux_row[:, 1:, 1:-1] - flux_row[:, :-1, 1:-1]) + (flux_column[:, 1:-1, 1:] - flux_column[:, 1:-1, :-1])
    hyper_zonal = diffuse(diffuse(zonal, unit_rows, unit_columns), inner_rows, inner_columns)
    hyper_meridional = diffuse(diffuse(meridional, unit_rows, unit_columns), inner_rows, inner_columns)
    core_mask = wet_cell_indicator[2:-2, 2:-2]
    rotation = planetary_spin_parameter[:, None]
    zonal_core = zonal[:, 2:-2, 2:-2]
    meridional_core = meridional[:, 2:-2, 2:-2]
    tracer_core = tracer[:, 2:-2, 2:-2]
    easting_current_next = core_mask * (zonal_core + rotation * meridional_core - pressure_coef * grad_row + diffuse(zonal_inner, visc_rows, visc_columns) - biharmonic_coef * hyper_zonal)
    poleward_current_next = core_mask * (meridional_core - rotation * zonal_core - pressure_coef * grad_column + diffuse(meridional_inner, visc_rows, visc_columns) - biharmonic_coef * hyper_meridional)
    tracer_next = core_mask * (tracer_core - advection_coef * spread + diffuse(tracer_inner, visc_rows, visc_columns))
    return easting_current_next, poleward_current_next, tracer_next


def surface_setup(padded_zonal, padded_meridional, padded_depth, sea_level_elevation, wet_cell_indicator):
    row_faces, column_faces = faces(wet_cell_indicator, padded_depth)
    core_mask = wet_cell_indicator[1:-1, 1:-1]
    diverge = 0.5 * (padded_zonal[2:, 1:-1] - padded_zonal[:-2, 1:-1]) + 0.5 * (padded_meridional[1:-1, 2:] - padded_meridional[1:-1, :-2])
    right_side = core_mask * (surface_coef * sea_level_elevation - divergence_coef * diverge)
    scaling = surface_coef + row_faces[1:, 1:-1] + row_faces[:-1, 1:-1] + column_faces[1:-1, 1:] + column_faces[1:-1, :-1]
    return row_faces, column_faces, right_side, scaling


def operate(padded_values, row_faces, column_faces):
    return surface_coef * padded_values[1:-1, 1:-1] - diffuse(padded_values, row_faces, column_faces)


def conjugate(right_side, scaling, row_faces, column_faces):
    solution = jnp.zeros_like(right_side)
    residual = right_side
    scaled = residual / scaling
    direction = scaled
    residual_dot = jnp.sum(residual * scaled)
    for iteration in range(ITERS):
        image = operate(jnp.pad(direction, 1), row_faces, column_faces)
        step_size = residual_dot / jnp.sum(direction * image)
        solution = solution + step_size * direction
        residual = residual - step_size * image
        if iteration + 1 < ITERS:
            scaled = residual / scaling
            dot_next = jnp.sum(residual * scaled)
            direction = scaled + (dot_next / residual_dot) * direction
            residual_dot = dot_next
    return solution, residual


def reference(easting_current, poleward_current, thermal_anomaly, planetary_spin_parameter, stratum_spacings, sideways_diffusivity, bathymetry_multiplier, sea_level_elevation, wet_dry_indicator):
    wet_cell_indicator = ocean_cells(wet_dry_indicator, 0, 0, MESH_Y_EXTENT, MESH_X_EXTENT, 2)
    bundled_arrays = jnp.concatenate([easting_current, poleward_current, thermal_anomaly, sideways_diffusivity[None]], axis=0)
    haloed_array = jnp.pad(bundled_arrays, ((0, 0), (2, 2), (2, 2)))
    easting_current_next, poleward_current_next, thermal_anomaly_next = stratified_advance(haloed_array, wet_cell_indicator, planetary_spin_parameter, stratum_spacings)
    thickness = stratum_spacings[:, None, None]
    transport_u = jnp.sum(easting_current_next * thickness, axis=0)
    transport_v = jnp.sum(poleward_current_next * thickness, axis=0)
    row_faces, column_faces, right_side, scaling = surface_setup(jnp.pad(transport_u, 1), jnp.pad(transport_v, 1), jnp.pad(bathymetry_multiplier, 1), sea_level_elevation, wet_cell_indicator[1:-1, 1:-1])
    barotropic_guess, equation_misfit = conjugate(right_side, scaling, row_faces, column_faces)
    return easting_current_next, poleward_current_next, thermal_anomaly_next, barotropic_guess, equation_misfit
```

```python
import functools

import jax
import jax.numpy as jnp
from jax import lax
from jax.experimental import pallas as pl
from jax.experimental.pallas import tpu as pltpu
from jax.sharding import PartitionSpec as P

TS = 64
ITERS = 3
CHUNKS = 4
HALO = 8

pressure_coef = 0.02
biharmonic_coef = 0.02
advection_coef = 0.5
surface_coef = 0.5
divergence_coef = 0.1

MESH = pl.DeviceIdType.MESH


def kernel(
    count,
    u_ref, v_ref, t_ref, spin_ref, thick_ref, visc_ref, depth_ref, sea_ref, wet_ref,
    ou_ref, ov_ref, ot_ref, ox_ref, or_ref,
    own, own2, buf, buf2, res, res2, weights, total, gathered,
    load_sem, load2_sem, local_sem, swap_send, swap_recv, halo_send, halo_recv,
    out_sem, back_send, back_recv, gram_send, gram_recv,
):
    levels, rows, columns = u_ref.shape
    half = rows // 2
    span = half + 2 * HALO
    reach = half + HALO
    per = levels // CHUNKS
    group = lax.axis_index("group")
    gx = lax.axis_index("gx")
    core = lax.axis_index("gy")
    other = 1 - core
    peers = 2 * count
    me = gx * 2 + core

    barrier = pltpu.get_barrier_semaphore()

    def greet(k, _):
        peer = lax.rem(me + k, peers)
        pl.semaphore_signal(
            barrier, inc=1, device_id=(group, peer // 2, lax.rem(peer, 2)), device_id_type=MESH
        )
        return 0

    lax.fori_loop(1, peers, greet, 0)

    def loads(k):
        part = pl.ds(k * per, per)
        return [
            pltpu.make_async_copy(ref.at[part], own.at[f, part], load_sem.at[f, k])
            for f, ref in enumerate((u_ref, v_ref, t_ref))
        ]

    flat_loads = [
        pltpu.make_async_copy(ref, own2.at[f], load2_sem.at[f])
        for f, ref in enumerate((visc_ref, depth_ref, sea_ref))
    ]
    for copy in flat_loads:
        copy.start()
    for k in range(CHUNKS):
        for copy in loads(k):
            copy.start()

    spin_row = jnp.broadcast_to(spin_ref[...], (rows, rows))
    diagonal = lax.broadcasted_iota(jnp.int32, (rows, rows), 0) == lax.broadcasted_iota(
        jnp.int32, (rows, rows), 1
    )
    spin_column = jnp.sum(jnp.where(diagonal, spin_row, 0.0), axis=1, keepdims=True)
    own2[3] = jnp.broadcast_to(spin_column, (rows, columns))

    first = gx == 0
    last = gx == count - 1

    def clear(start):
        def one(l, _):
            for h in range(2):
                for f in range(3):
                    buf[h, f, l, start : start + HALO, :] = jnp.zeros((HALO, columns), jnp.float32)
            return 0

        lax.fori_loop(0, levels, one, 0)
        for h in range(2):
            for f in range(4):
                buf2[h, f, start : start + HALO, :] = jnp.zeros((HALO, columns), jnp.float32)

    @pl.when(jnp.logical_and(first, core == 0))
    def _():
        clear(0)

    @pl.when(jnp.logical_and(last, core == 1))
    def _():
        clear(HALO + half)

    pl.semaphore_wait(barrier, peers - 1)

    def source(k, where):
        if k is None:
            return own2.at[:, where, :]
        return own.at[:, pl.ds(k * per, per), where, :]

    def target(k, which, where):
        if k is None:
            return buf2.at[which, :, where, :]
        return buf.at[which, :, pl.ds(k * per, per), where, :]

    def slot(k):
        return CHUNKS if k is None else k

    def taken(c):
        return pl.ds(pl.multiple_of((half - HALO) * c, 8), reach)

    def placed(c):
        return pl.ds(pl.multiple_of(HALO - HALO * c, 8), reach)

    def swap(k):
        return pltpu.make_async_remote_copy(
            src_ref=source(k, taken(other)),
            dst_ref=target(k, core, placed(other)),
            send_sem=swap_send.at[slot(k)],
            recv_sem=swap_recv.at[slot(k)],
            device_id=(group, gx, other),
            device_id_type=MESH,
        )

    def keep(k):
        return pltpu.make_async_copy(
            source(k, taken(core)), target(k, core, placed(core)), local_sem.at[slot(k)]
        )

    def halo_down(k):
        return pltpu.make_async_remote_copy(
            src_ref=source(k, pl.ds(rows - HALO, HALO)),
            dst_ref=target(k, core, pl.ds(0, HALO)),
            send_sem=halo_send.at[0, slot(k)],
            recv_sem=halo_recv.at[core, slot(k)],
            device_id=(group, lax.rem(gx + 1, count), 0),
            device_id_type=MESH,
        )

    def halo_up(k):
        return pltpu.make_async_remote_copy(
            src_ref=source(k, pl.ds(0, HALO)),
            dst_ref=target(k, core, pl.ds(HALO + half, HALO)),
            send_sem=halo_send.at[1, slot(k)],
            recv_sem=halo_recv.at[core, slot(k)],
            device_id=(group, lax.rem(gx + count - 1, count), 1),
            device_id_type=MESH,
        )

    def halo_in(k, h):
        return pltpu.make_async_remote_copy(
            src_ref=source(k, pl.ds(0, HALO)),
            dst_ref=target(k, h, pl.ds(0, HALO)),
            send_sem=halo_send.at[0, slot(k)],
            recv_sem=halo_recv.at[h, slot(k)],
            device_id=(group, gx, other),
            device_id_type=MESH,
        )

    has_outer = jnp.where(core == 0, gx > 0, gx < count - 1)

    def send(k):
        @pl.when(gx < count - 1)
        def _():
            halo_down(k).start()

        @pl.when(gx > 0)
        def _():
            halo_up(k).start()

        swap(k).start()
        keep(k).start()

    def arrive(k):
        keep(k).wait()
        swap(k).wait_recv()

        @pl.when(has_outer)
        def _():
            halo_in(k, 0).wait_recv()
            halo_in(k, 1).wait_recv()

    def sent(k):
        swap(k).wait_send()

        @pl.when(gx < count - 1)
        def _():
            halo_down(k).wait_send()

        @pl.when(gx > 0)
        def _():
            halo_up(k).wait_send()

    for copy in flat_loads:
        copy.wait()
    send(None)
    for k in range(CHUNKS):
        for copy in loads(k):
            copy.wait()
        send(k)

    lane = lax.broadcasted_iota(jnp.int32, (span, columns), 1)
    row = lax.broadcasted_iota(jnp.int32, (span, columns), 0)
    at_left = lane == 0
    at_right = lane == columns - 1

    def up(a):
        return pltpu.roll(a, 1, 0)

    def down(a):
        return pltpu.roll(a, span - 1, 0)

    def left(pair):
        r0, r1 = [pltpu.roll(a, 1, 1) for a in pair]
        return [jnp.where(at_left, 0.0, r0), jnp.where(at_left, r0, r1)]

    def right(pair):
        r0, r1 = [pltpu.roll(a, columns - 1, 1) for a in pair]
        return [jnp.where(at_right, r1, r0), jnp.where(at_right, 0.0, r1)]

    def around(pair):
        return [up(a) for a in pair], [down(a) for a in pair], left(pair), right(pair)

    outer_tile = jnp.where(core == 0, gx - 1, gx + 1)
    outer_tile_safe = jnp.clip(outer_tile, 0, count - 1)
    outer_flag = jnp.where(has_outer, 1, 0)
    in_outer = jnp.where(core == 0, row, span - 1 - row) < HALO
    mask = []
    for h in range(2):
        inner = jnp.where(lane < TS, wet_ref[gx, 2 * h], wet_ref[gx, 2 * h + 1])
        outer = jnp.where(
            lane < TS,
            wet_ref[outer_tile_safe, 2 * h] * outer_flag,
            wet_ref[outer_tile_safe, 2 * h + 1] * outer_flag,
        )
        mask.append(jnp.where(in_outer, outer, inner).astype(jnp.float32))
    sides = around(mask)
    for h in range(2):
        m = mask[h]
        mu, md, ml, mr = [side[h] for side in sides]
        number = mu + md + ml + mr
        weights[h, 0] = m
        weights[h, 1] = number
        weights[h, 2] = mu
        weights[h, 3] = md
        weights[h, 4] = ml
        weights[h, 5] = mr
        weights[h, 6] = mu - md
        weights[h, 7] = ml - mr

    arrive(None)

    def face_weights(pair):
        ring = around(pair)
        result = []
        for h in range(2):
            four = [
                0.5 * (pair[h] + ring[side][h]) * mask[h] * sides[side][h] for side in range(4)
            ]
            result.append(four)
        return result

    viscous = face_weights([buf2[0, 0], buf2[1, 0]])
    for h in range(2):
        for side in range(4):
            weights[h, 8 + side] = viscous[h][side]
        weights[h, 12] = viscous[h][0] + viscous[h][1] + viscous[h][2] + viscous[h][3]

    for h in range(2):
        for i in range(4):
            total[h, i] = jnp.zeros((span, columns), jnp.float32)

    def level(l, _):
        thickness = thick_ref[l]
        fields = []
        rings = []
        for f in range(3):
            pair = [buf[h, f, l] * weights[h, 0] for h in range(2)]
            fields.append(pair)
            rings.append(around(pair))
        u, v, t = fields
        viscous_part = []
        for f in range(3):
            viscous_part.append(
                [
                    weights[h, 8] * rings[f][0][h]
                    + weights[h, 9] * rings[f][1][h]
                    + (weights[h, 10] * rings[f][2][h] + weights[h, 11] * rings[f][3][h])
                    - weights[h, 12] * fields[f][h]
                    for h in range(2)
                ]
            )
        hyper = []
        for f in range(2):
            once = [
                weights[h, 0]
                * (
                    (rings[f][0][h] + rings[f][1][h])
                    + (rings[f][2][h] + rings[f][3][h])
                    - weights[h, 1] * fields[f][h]
                )
                for h in range(2)
            ]
            ring = around(once)
            hyper.append(
                [
                    (ring[0][h] + ring[1][h]) + (ring[2][h] + ring[3][h]) - weights[h, 1] * once[h]
                    for h in range(2)
                ]
            )
        tu, td, tl, tr = rings[2]
        uu, ud, _, _ = rings[0]
        _, _, vl, vr = rings[1]
        for h in range(2):
            m = weights[h, 0]
            slope_row = thickness * (td[h] - tu[h] + weights[h, 6] * t[h])
            slope_column = thickness * (tr[h] - tl[h] + weights[h, 7] * t[h])
            sum_row = total[h, 2] + slope_row
            sum_column = total[h, 3] + slope_column
            total[h, 2] = sum_row
            total[h, 3] = sum_column
            grad_row = sum_row - 0.5 * slope_row
            grad_column = sum_column - 0.5 * slope_column
            spread = (
                weights[h, 3] * ((u[h] + ud[h]) * (t[h] + td[h]))
                - weights[h, 2] * ((u[h] + uu[h]) * (t[h] + tu[h]))
                + (
                    weights[h, 5] * ((v[h] + vr[h]) * (t[h] + tr[h]))
                    - weights[h, 4] * ((v[h] + vl[h]) * (t[h] + tl[h]))
                )
            )
            spin = buf2[h, 3]
            u_next = m * (
                u[h]
                + spin * v[h]
                - (0.5 * pressure_coef) * grad_row
                + viscous_part[0][h]
                - biharmonic_coef * hyper[0][h]
            )
            v_next = m * (
                v[h]
                - spin * u[h]
                - (0.5 * pressure_coef) * grad_column
                + viscous_part[1][h]
                - biharmonic_coef * hyper[1][h]
            )
            t_next = m * (t[h] - (0.25 * advection_coef) * spread + viscous_part[2][h])
            total[h, 0] += thickness * u_next
            total[h, 1] += thickness * v_next
            res[h, 0, l] = u_next[HALO : HALO + half]
            res[h, 1, l] = v_next[HALO : HALO + half]
            res[h, 2, l] = t_next[HALO : HALO + half]
        return 0

    mine = pl.ds(pl.multiple_of(half * core, 8), half)

    def outs(k):
        part = pl.ds(k * per, per)
        local = [
            pltpu.make_async_copy(
                res.at[core, f, part], ref.at[part, mine, :], out_sem.at[f, k]
            )
            for f, ref in enumerate((ou_ref, ov_ref, ot_ref))
        ]
        remote = [
            pltpu.make_async_remote_copy(
                src_ref=res.at[other, f, part],
                dst_ref=ref.at[part, mine, :],
                send_sem=back_send.at[f, k],
                recv_sem=back_recv.at[f, k],
                device_id=(group, gx, other),
                device_id_type=MESH,
            )
            for f, ref in enumerate((ou_ref, ov_ref, ot_ref))
        ]
        return remote + local

    def chunk(k, _):
        arrive(k)
        lax.fori_loop(k * per, (k + 1) * per, level, 0)
        for copy in outs(k):
            copy.start()
        return 0

    lax.fori_loop(0, CHUNKS, chunk, 0)

    face = face_weights([buf2[0, 1], buf2[1, 1]])
    scaling = [
        surface_coef + (face[h][0] + face[h][1]) + (face[h][2] + face[h][3]) for h in range(2)
    ]
    inverse = [1.0 / scaling[h] for h in range(2)]
    flow_u = [total[h, 0] for h in range(2)]
    flow_v = [total[h, 1] for h in range(2)]
    before, after = left(flow_v), right(flow_v)
    vectors = [
        [
            mask[h]
            * (
                surface_coef * buf2[h, 2]
                - (0.5 * divergence_coef)
                * ((down(flow_u[h]) - up(flow_u[h])) + (after[h] - before[h]))
            )
            * inverse[h]
            for h in range(2)
        ]
    ]
    for _ in range(ITERS):
        ring = around(vectors[-1])
        vectors.append(
            [
                (
                    (face[h][0] * ring[0][h] + face[h][1] * ring[1][h])
                    + (face[h][2] * ring[2][h] + face[h][3] * ring[3][h])
                )
                * inverse[h]
                for h in range(2)
            ]
        )
    inside = slice(HALO, HALO + half)
    basis = [[pair[h][inside] for h in range(2)] for pair in vectors]
    scale = [scaling[h][inside] for h in range(2)]

    def dot(a, b):
        both = scale[0] * a[0] * b[0] + scale[1] * a[1] * b[1]
        return jnp.sum(both, axis=0, keepdims=True)

    moments = 2 * ITERS - 1
    difference = [
        [basis[k][h] - basis[k + 1][h] for h in range(2)] for k in range(ITERS)
    ]
    gathered[me] = jnp.zeros(gathered.shape[1:], jnp.float32)
    lines = [dot(basis[(k + 1) // 2], basis[k // 2]) for k in range(moments)]
    lines += [dot(basis[(k + 1) // 2], difference[k // 2]) for k in range(moments)]
    for k, line in enumerate(lines):
        gathered[me, k : k + 1, :] = line

    def gram(k):
        peer = lax.rem(me + k, peers)
        return pltpu.make_async_remote_copy(
            src_ref=gathered.at[me],
            dst_ref=gathered.at[me],
            send_sem=gram_send.at[k],
            recv_sem=gram_recv.at[me],
            device_id=(group, peer // 2, lax.rem(peer, 2)),
            device_id_type=MESH,
        )

    def gram_from(k):
        peer = lax.rem(me + k, peers)
        return pltpu.make_async_remote_copy(
            src_ref=gathered.at[peer],
            dst_ref=gathered.at[peer],
            send_sem=gram_send.at[k],
            recv_sem=gram_recv.at[peer],
            device_id=(group, peer // 2, lax.rem(peer, 2)),
            device_id_type=MESH,
        )

    def gram_start(k, _):
        gram(k).start()
        return 0

    def gram_wait(k, _):
        gram_from(k).wait_recv()
        return 0

    def gram_sent(k, _):
        gram(k).wait_send()
        return 0

    lax.fori_loop(1, peers, gram_start, 0)
    lax.fori_loop(1, peers, gram_wait, 0)

    summed = lax.fori_loop(
        0, peers, lambda k, acc: acc + gathered[k], jnp.zeros(gathered.shape[1:], jnp.float32)
    )
    sums = jnp.sum(summed, axis=1, keepdims=True)
    mass = [sums[k : k + 1] for k in range(moments)]
    stiff = [sums[moments + k : moments + k + 1] for k in range(moments)]

    def quadratic(coefs, table):
        value = None
        for i, a in enumerate(coefs):
            for j, b in enumerate(coefs):
                term = a * b * table[i + j]
                value = term if value is None else value + term
        return value

    one = jnp.ones((1, 1), jnp.float32)
    zero = jnp.zeros((1, 1), jnp.float32)
    remains = [one]
    heading = [one]
    guess = [zero] * ITERS
    rho = mass[0]
    for iteration in range(ITERS):
        step = rho / quadratic(heading, stiff)
        for j, c in enumerate(heading):
            guess[j] = guess[j] + step * c
        moved = remains + [zero]
        for j, c in enumerate(heading):
            moved[j] = moved[j] - step * c
            moved[j + 1] = moved[j + 1] + step * c
        remains = moved
        if iteration + 1 < ITERS:
            rho_new = quadratic(remains, mass)
            ratio = rho_new / rho
            heading = [
                remains[j] + ratio * heading[j] if j < len(heading) else remains[j]
                for j in range(len(remains))
            ]
            rho = rho_new

    for h in range(2):
        x = guess[0] * basis[0][h]
        for j in range(1, ITERS):
            x = x + guess[j] * basis[j][h]
        r = remains[0] * basis[0][h]
        for j in range(1, ITERS + 1):
            r = r + remains[j] * basis[j][h]
        res2[h, 0] = x
        res2[h, 1] = scale[h] * r

    def flat_outs():
        k = CHUNKS
        local = [
            pltpu.make_async_copy(res2.at[core, f], ref.at[mine, :], out_sem.at[f, k])
            for f, ref in enumerate((ox_ref, or_ref))
        ]
        remote = [
            pltpu.make_async_remote_copy(
                src_ref=res2.at[other, f],
                dst_ref=ref.at[mine, :],
                send_sem=back_send.at[f, k],
                recv_sem=back_recv.at[f, k],
                device_id=(group, gx, other),
                device_id_type=MESH,
            )
            for f, ref in enumerate((ox_ref, or_ref))
        ]
        return remote + local

    for copy in flat_outs():
        copy.start()
    lax.fori_loop(1, peers, gram_sent, 0)
    sent(None)
    for k in range(CHUNKS):
        sent(k)
        for copy in outs(k):
            copy.wait()
    for copy in flat_outs():
        copy.wait()


def per_device(count, *args):
    u, v, t, spin, thick, visc, depth, sea, wet = args
    levels, rows, columns = u.shape
    half = rows // 2
    span = half + 2 * HALO
    assert rows == TS and columns == 2 * TS
    peers = 2 * count
    f32 = jnp.float32
    anywhere = pl.BlockSpec(memory_space=pl.ANY)
    vmem = pl.BlockSpec(memory_space=pltpu.VMEM)
    smem = pl.BlockSpec(memory_space=pltpu.SMEM)
    dma = pltpu.SemaphoreType.DMA
    return pl.pallas_call(
        functools.partial(kernel, count),
        out_shape=[jax.ShapeDtypeStruct(u.shape, f32)] * 3
        + [jax.ShapeDtypeStruct(sea.shape, f32)] * 2,
        in_specs=[anywhere, anywhere, anywhere, vmem, smem, anywhere, anywhere, anywhere, smem],
        out_specs=[anywhere] * 5,
        scratch_shapes=[
            pltpu.VMEM((3, levels, rows, columns), f32),
            pltpu.VMEM((4, rows, columns), f32),
            pltpu.VMEM((2, 3, levels, span, columns), f32),
            pltpu.VMEM((2, 4, span, columns), f32),
            pltpu.VMEM((2, 3, levels, half, columns), f32),
            pltpu.VMEM((2, 2, half, columns), f32),
            pltpu.VMEM((2, 13, span, columns), f32),
            pltpu.VMEM((2, 4, span, columns), f32),
            pltpu.VMEM((peers, 16, columns), f32),
            dma((3, CHUNKS)),
            dma((3,)),
            dma((CHUNKS + 1,)),
            dma((CHUNKS + 1,)),
            dma((CHUNKS + 1,)),
            dma((2, CHUNKS + 1)),
            dma((2, CHUNKS + 1)),
            dma((3, CHUNKS + 1)),
            dma((3, CHUNKS + 1)),
            dma((3, CHUNKS + 1)),
            dma((peers,)),
            dma((peers,)),
        ],
        compiler_params=pltpu.CompilerParams(
            collective_id=0, has_side_effects=True, vmem_limit_bytes=32 * 1024 * 1024
        ),
    )(u, v, t, spin.reshape(1, rows), thick, visc, depth, sea, wet)


def solution(mesh):
    cells = P(None, ("group", "gx"), "gy")
    flat = P(("group", "gx"), "gy")
    assert mesh.shape["gy"] == 2
    return jax.shard_map(
        functools.partial(per_device, mesh.shape["gx"]),
        mesh=mesh,
        in_specs=(cells, cells, cells, P("gx"), P(), P("gx", "gy"), P("gx", "gy"), flat, P()),
        out_specs=(cells, cells, cells, flat, flat),
        check_vma=False,
    )
```

```python
import functools

import jax
import jax.numpy as jnp
from jax import lax
from jax.experimental import pallas as pl
from jax.experimental.pallas import tpu as pltpu
from jax.sharding import PartitionSpec as P

TS = 64
ITERS = 3
CHUNKS = 4
HALO = 8
VMEM_BYTES = 60 * 1024 * 1024

pressure_coef = 0.02
biharmonic_coef = 0.02
advection_coef = 0.5
surface_coef = 0.5
divergence_coef = 0.1

MESH = pl.DeviceIdType.MESH


def kernel(
    count,
    u_ref, v_ref, t_ref, spin_ref, thick_ref, visc_ref, depth_ref, sea_ref, wet_ref,
    ou_ref, ov_ref, ot_ref, ox_ref, or_ref,
    own_spin, buf, buf2, res, res2, weights, total, gathered,
    local_sem, swap_send, swap_recv, halo_send, halo_recv,
    out_sem, back_send, back_recv, gram_send, gram_recv,
):
    levels, rows, columns = u_ref.shape
    half = rows // 2
    span = half + 2 * HALO
    reach = half + HALO
    per = levels // CHUNKS
    group = lax.axis_index("group")
    gx = lax.axis_index("gx")
    core = lax.axis_index("gy")
    other = 1 - core
    peers = 2 * count
    me = gx * 2 + core

    barrier = pltpu.get_barrier_semaphore()

    def greet(k, _):
        peer = lax.rem(me + k, peers)
        pl.semaphore_signal(
            barrier, inc=1, device_id=(group, peer // 2, lax.rem(peer, 2)), device_id_type=MESH
        )
        return 0

    lax.fori_loop(1, peers, greet, 0)

    spin_row = jnp.broadcast_to(spin_ref[...], (rows, rows))
    diagonal = lax.broadcasted_iota(jnp.int32, (rows, rows), 0) == lax.broadcasted_iota(
        jnp.int32, (rows, rows), 1
    )
    spin_column = jnp.sum(jnp.where(diagonal, spin_row, 0.0), axis=1, keepdims=True)
    own_spin[...] = jnp.broadcast_to(spin_column, (rows, columns))

    def taken(c):
        return pl.ds(pl.multiple_of((half - HALO) * c, 8), reach)

    def placed(c):
        return pl.ds(pl.multiple_of(HALO - HALO * c, 8), reach)

    has_outer = jnp.where(core == 0, gx > 0, gx < count - 1)
    cells = (u_ref, v_ref, t_ref)
    flats = (visc_ref, depth_ref, sea_ref, own_spin)

    def source(f, k, where):
        if k is None:
            return flats[f].at[where, :]
        return cells[f].at[pl.ds(k * per, per), where, :]

    def target(f, k, which, where):
        if k is None:
            return buf2.at[which, f, where, :]
        return buf.at[which, f, pl.ds(k * per, per), where, :]

    def slot(k):
        return CHUNKS if k is None else k

    def swap(f, k):
        return pltpu.make_async_remote_copy(
            src_ref=source(f, k, taken(other)),
            dst_ref=target(f, k, core, placed(other)),
            send_sem=swap_send.at[f, slot(k)],
            recv_sem=swap_recv.at[f, slot(k)],
            device_id=(group, gx, other),
            device_id_type=MESH,
        )

    def keep(f, k):
        return pltpu.make_async_copy(
            source(f, k, taken(core)),
            target(f, k, core, placed(core)),
            local_sem.at[f, slot(k)],
        )

    def halo_down(f, k):
        return pltpu.make_async_remote_copy(
            src_ref=source(f, k, pl.ds(rows - HALO, HALO)),
            dst_ref=target(f, k, core, pl.ds(0, HALO)),
            send_sem=halo_send.at[0, f, slot(k)],
            recv_sem=halo_recv.at[core, f, slot(k)],
            device_id=(group, lax.rem(gx + 1, count), 0),
            device_id_type=MESH,
        )

    def halo_up(f, k):
        return pltpu.make_async_remote_copy(
            src_ref=source(f, k, pl.ds(0, HALO)),
            dst_ref=target(f, k, core, pl.ds(HALO + half, HALO)),
            send_sem=halo_send.at[1, f, slot(k)],
            recv_sem=halo_recv.at[core, f, slot(k)],
            device_id=(group, lax.rem(gx + count - 1, count), 1),
            device_id_type=MESH,
        )

    def halo_in(f, k, h):
        return pltpu.make_async_remote_copy(
            src_ref=source(f, k, pl.ds(0, HALO)),
            dst_ref=target(f, k, h, pl.ds(0, HALO)),
            send_sem=halo_send.at[0, f, slot(k)],
            recv_sem=halo_recv.at[h, f, slot(k)],
            device_id=(group, gx, other),
            device_id_type=MESH,
        )

    def span_of(k):
        return range(4) if k is None else range(3)

    def send_halo(k):
        @pl.when(gx < count - 1)
        def _():
            for f in span_of(k):
                halo_down(f, k).start()

        @pl.when(gx > 0)
        def _():
            for f in span_of(k):
                halo_up(f, k).start()

    def send_swap(k):
        for f in range(3):
            swap(f, k).start()

    def arrive(k):
        for f in range(3):
            keep(f, k).wait()
            swap(f, k).wait_recv()

        @pl.when(has_outer)
        def _():
            for f in span_of(k):
                halo_in(f, k, 0).wait_recv()
                halo_in(f, k, 1).wait_recv()

    def sent(k):
        for f in range(3):
            swap(f, k).wait_send()

        @pl.when(gx < count - 1)
        def _():
            for f in span_of(k):
                halo_down(f, k).wait_send()

        @pl.when(gx > 0)
        def _():
            for f in span_of(k):
                halo_up(f, k).wait_send()

    everything = [None] + list(range(CHUNKS))
    for k in everything:
        for f in range(3):
            keep(f, k).start()
    own_rows = own_spin[taken(core), :]
    for h in range(2):
        buf2[h, 3, placed(core), :] = own_rows
    first = gx == 0
    last = gx == count - 1

    def clear(start):
        def one(l, _):
            for h in range(2):
                for f in range(3):
                    buf[h, f, l, start : start + HALO, :] = jnp.zeros((HALO, columns), jnp.float32)
            return 0

        lax.fori_loop(0, levels, one, 0)
        for h in range(2):
            for f in range(4):
                buf2[h, f, start : start + HALO, :] = jnp.zeros((HALO, columns), jnp.float32)

    @pl.when(jnp.logical_and(first, core == 0))
    def _():
        clear(0)

    @pl.when(jnp.logical_and(last, core == 1))
    def _():
        clear(HALO + half)

    pl.semaphore_wait(barrier, peers - 1)
    for k in everything:
        send_halo(k)
        send_swap(k)

    lane = lax.broadcasted_iota(jnp.int32, (span, columns), 1)
    row = lax.broadcasted_iota(jnp.int32, (span, columns), 0)
    at_left = lane == 0
    at_right = lane == columns - 1

    def up(a):
        return pltpu.roll(a, 1, 0)

    def down(a):
        return pltpu.roll(a, span - 1, 0)

    def left(pair):
        r0, r1 = [pltpu.roll(a, 1, 1) for a in pair]
        return [jnp.where(at_left, 0.0, r0), jnp.where(at_left, r0, r1)]

    def right(pair):
        r0, r1 = [pltpu.roll(a, columns - 1, 1) for a in pair]
        return [jnp.where(at_right, r1, r0), jnp.where(at_right, 0.0, r1)]

    def around(pair):
        return [up(a) for a in pair], [down(a) for a in pair], left(pair), right(pair)

    outer_tile = jnp.where(core == 0, gx - 1, gx + 1)
    outer_tile_safe = jnp.clip(outer_tile, 0, count - 1)
    outer_flag = jnp.where(has_outer, 1, 0)
    in_outer = jnp.where(core == 0, row, span - 1 - row) < HALO
    mask = []
    for h in range(2):
        inner = jnp.where(lane < TS, wet_ref[2 * h, gx], wet_ref[2 * h + 1, gx])
        outer = jnp.where(
            lane < TS,
            wet_ref[2 * h, outer_tile_safe] * outer_flag,
            wet_ref[2 * h + 1, outer_tile_safe] * outer_flag,
        )
        mask.append(jnp.where(in_outer, outer, inner).astype(jnp.float32))
    sides = around(mask)
    for h in range(2):
        m = mask[h]
        mu, md, ml, mr = [side[h] for side in sides]
        number = mu + md + ml + mr
        weights[h, 0] = m
        weights[h, 1] = number
        weights[h, 2] = mu
        weights[h, 3] = md
        weights[h, 4] = ml
        weights[h, 5] = mr
        weights[h, 6] = mu - md
        weights[h, 7] = ml - mr

    arrive(None)

    def face_weights(pair):
        ring = around(pair)
        result = []
        for h in range(2):
            four = [
                0.5 * (pair[h] + ring[side][h]) * mask[h] * sides[side][h] for side in range(4)
            ]
            result.append(four)
        return result

    viscous = face_weights([buf2[0, 0], buf2[1, 0]])
    for h in range(2):
        for side in range(4):
            weights[h, 8 + side] = viscous[h][side]
        weights[h, 12] = viscous[h][0] + viscous[h][1] + viscous[h][2] + viscous[h][3]

    for h in range(2):
        for i in range(4):
            total[h, i] = jnp.zeros((span, columns), jnp.float32)

    def level(l, _):
        thickness = thick_ref[l]
        fields = []
        rings = []
        for f in range(3):
            pair = [buf[h, f, l] * weights[h, 0] for h in range(2)]
            fields.append(pair)
            rings.append(around(pair))
        u, v, t = fields
        viscous_part = []
        for f in range(3):
            viscous_part.append(
                [
                    weights[h, 8] * rings[f][0][h]
                    + weights[h, 9] * rings[f][1][h]
                    + (weights[h, 10] * rings[f][2][h] + weights[h, 11] * rings[f][3][h])
                    - weights[h, 12] * fields[f][h]
                    for h in range(2)
                ]
            )
        hyper = []
        for f in range(2):
            once = [
                weights[h, 0]
                * (
                    (rings[f][0][h] + rings[f][1][h])
                    + (rings[f][2][h] + rings[f][3][h])
                    - weights[h, 1] * fields[f][h]
                )
                for h in range(2)
            ]
            ring = around(once)
            hyper.append(
                [
                    (ring[0][h] + ring[1][h]) + (ring[2][h] + ring[3][h]) - weights[h, 1] * once[h]
                    for h in range(2)
                ]
            )
        tu, td, tl, tr = rings[2]
        uu, ud, _, _ = rings[0]
        _, _, vl, vr = rings[1]
        for h in range(2):
            m = weights[h, 0]
            slope_row = thickness * (td[h] - tu[h] + weights[h, 6] * t[h])
            slope_column = thickness * (tr[h] - tl[h] + weights[h, 7] * t[h])
            sum_row = total[h, 2] + slope_row
            sum_column = total[h, 3] + slope_column
            total[h, 2] = sum_row
            total[h, 3] = sum_column
            grad_row = sum_row - 0.5 * slope_row
            grad_column = sum_column - 0.5 * slope_column
            spread = (
                weights[h, 3] * ((u[h] + ud[h]) * (t[h] + td[h]))
                - weights[h, 2] * ((u[h] + uu[h]) * (t[h] + tu[h]))
                + (
                    weights[h, 5] * ((v[h] + vr[h]) * (t[h] + tr[h]))
                    - weights[h, 4] * ((v[h] + vl[h]) * (t[h] + tl[h]))
                )
            )
            spin = buf2[h, 3]
            u_next = m * (
                u[h]
                + spin * v[h]
                - (0.5 * pressure_coef) * grad_row
                + viscous_part[0][h]
                - biharmonic_coef * hyper[0][h]
            )
            v_next = m * (
                v[h]
                - spin * u[h]
                - (0.5 * pressure_coef) * grad_column
                + viscous_part[1][h]
                - biharmonic_coef * hyper[1][h]
            )
            t_next = m * (t[h] - (0.25 * advection_coef) * spread + viscous_part[2][h])
            total[h, 0] += thickness * u_next
            total[h, 1] += thickness * v_next
            res[h, 0, l] = u_next[HALO : HALO + half]
            res[h, 1, l] = v_next[HALO : HALO + half]
            res[h, 2, l] = t_next[HALO : HALO + half]
        return 0

    mine = pl.ds(pl.multiple_of(half * core, 8), half)

    def outs(k):
        part = pl.ds(k * per, per)
        local = [
            pltpu.make_async_copy(
                res.at[core, f, part], ref.at[part, mine, :], out_sem.at[f, k]
            )
            for f, ref in enumerate((ou_ref, ov_ref, ot_ref))
        ]
        remote = [
            pltpu.make_async_remote_copy(
                src_ref=res.at[other, f, part],
                dst_ref=ref.at[part, mine, :],
                send_sem=back_send.at[f, k],
                recv_sem=back_recv.at[f, k],
                device_id=(group, gx, other),
                device_id_type=MESH,
            )
            for f, ref in enumerate((ou_ref, ov_ref, ot_ref))
        ]
        return remote + local

    def chunk(k, _):
        arrive(k)
        lax.fori_loop(k * per, (k + 1) * per, level, 0)
        for copy in outs(k):
            copy.start()
        return 0

    lax.fori_loop(0, CHUNKS, chunk, 0)

    face = face_weights([buf2[0, 1], buf2[1, 1]])
    scaling = [
        surface_coef + (face[h][0] + face[h][1]) + (face[h][2] + face[h][3]) for h in range(2)
    ]
    inverse = [1.0 / scaling[h] for h in range(2)]
    flow_u = [total[h, 0] for h in range(2)]
    flow_v = [total[h, 1] for h in range(2)]
    before, after = left(flow_v), right(flow_v)
    vectors = [
        [
            mask[h]
            * (
                surface_coef * buf2[h, 2]
                - (0.5 * divergence_coef)
                * ((down(flow_u[h]) - up(flow_u[h])) + (after[h] - before[h]))
            )
            * inverse[h]
            for h in range(2)
        ]
    ]
    for _ in range(ITERS):
        ring = around(vectors[-1])
        vectors.append(
            [
                (
                    (face[h][0] * ring[0][h] + face[h][1] * ring[1][h])
                    + (face[h][2] * ring[2][h] + face[h][3] * ring[3][h])
                )
                * inverse[h]
                for h in range(2)
            ]
        )
    inside = slice(HALO, HALO + half)
    basis = [[pair[h][inside] for h in range(2)] for pair in vectors]
    scale = [scaling[h][inside] for h in range(2)]

    def dot(a, b):
        both = scale[0] * a[0] * b[0] + scale[1] * a[1] * b[1]
        return jnp.sum(both, axis=0, keepdims=True)

    moments = 2 * ITERS - 1
    difference = [
        [basis[k][h] - basis[k + 1][h] for h in range(2)] for k in range(ITERS)
    ]
    gathered[me] = jnp.zeros(gathered.shape[1:], jnp.float32)
    lines = [dot(basis[(k + 1) // 2], basis[k // 2]) for k in range(moments)]
    lines += [dot(basis[(k + 1) // 2], difference[k // 2]) for k in range(moments)]
    for k, line in enumerate(lines):
        gathered[me, k : k + 1, :] = line

    def gram(k):
        peer = lax.rem(me + k, peers)
        return pltpu.make_async_remote_copy(
            src_ref=gathered.at[me],
            dst_ref=gathered.at[me],
            send_sem=gram_send.at[k],
            recv_sem=gram_recv.at[me],
            device_id=(group, peer // 2, lax.rem(peer, 2)),
            device_id_type=MESH,
        )

    def gram_from(k):
        peer = lax.rem(me + k, peers)
        return pltpu.make_async_remote_copy(
            src_ref=gathered.at[peer],
            dst_ref=gathered.at[peer],
            send_sem=gram_send.at[k],
            recv_sem=gram_recv.at[peer],
            device_id=(group, peer // 2, lax.rem(peer, 2)),
            device_id_type=MESH,
        )

    def gram_start(k, _):
        gram(k).start()
        return 0

    def gram_wait(k, _):
        gram_from(k).wait_recv()
        return 0

    def gram_sent(k, _):
        gram(k).wait_send()
        return 0

    lax.fori_loop(1, peers, gram_start, 0)
    lax.fori_loop(1, peers, gram_wait, 0)

    summed = lax.fori_loop(
        0, peers, lambda k, acc: acc + gathered[k], jnp.zeros(gathered.shape[1:], jnp.float32)
    )
    sums = jnp.sum(summed, axis=1, keepdims=True)
    mass = [sums[k : k + 1] for k in range(moments)]
    stiff = [sums[moments + k : moments + k + 1] for k in range(moments)]

    def quadratic(coefs, table):
        value = None
        for i, a in enumerate(coefs):
            for j, b in enumerate(coefs):
                term = a * b * table[i + j]
                value = term if value is None else value + term
        return value

    one = jnp.ones((1, 1), jnp.float32)
    zero = jnp.zeros((1, 1), jnp.float32)
    remains = [one]
    heading = [one]
    guess = [zero] * ITERS
    rho = mass[0]
    for iteration in range(ITERS):
        step = rho / quadratic(heading, stiff)
        for j, c in enumerate(heading):
            guess[j] = guess[j] + step * c
        moved = remains + [zero]
        for j, c in enumerate(heading):
            moved[j] = moved[j] - step * c
            moved[j + 1] = moved[j + 1] + step * c
        remains = moved
        if iteration + 1 < ITERS:
            rho_new = quadratic(remains, mass)
            ratio = rho_new / rho
            heading = [
                remains[j] + ratio * heading[j] if j < len(heading) else remains[j]
                for j in range(len(remains))
            ]
            rho = rho_new

    for h in range(2):
        x = guess[0] * basis[0][h]
        for j in range(1, ITERS):
            x = x + guess[j] * basis[j][h]
        r = remains[0] * basis[0][h]
        for j in range(1, ITERS + 1):
            r = r + remains[j] * basis[j][h]
        res2[h, 0] = x
        res2[h, 1] = scale[h] * r

    def flat_outs():
        k = CHUNKS
        local = [
            pltpu.make_async_copy(res2.at[core, f], ref.at[mine, :], out_sem.at[f, k])
            for f, ref in enumerate((ox_ref, or_ref))
        ]
        remote = [
            pltpu.make_async_remote_copy(
                src_ref=res2.at[other, f],
                dst_ref=ref.at[mine, :],
                send_sem=back_send.at[f, k],
                recv_sem=back_recv.at[f, k],
                device_id=(group, gx, other),
                device_id_type=MESH,
            )
            for f, ref in enumerate((ox_ref, or_ref))
        ]
        return remote + local

    for copy in flat_outs():
        copy.start()
    lax.fori_loop(1, peers, gram_sent, 0)
    sent(None)
    for k in range(CHUNKS):
        sent(k)
        for copy in outs(k):
            copy.wait()
    for copy in flat_outs():
        copy.wait()


def deliver(*refs):
    sources, targets, held = refs[:5], refs[5:10], refs[10:15]
    into_sem, out_sem = refs[15:]

    def cut(ref, k):
        size = ref.shape[0] // CHUNKS
        return ref.at[pl.ds(k * size, size)]

    pieces = [(i, k) for k in range(CHUNKS) for i in range(5)]
    into = [
        pltpu.make_async_copy(cut(sources[i], k), cut(held[i], k), into_sem.at[i, k])
        for i, k in pieces
    ]
    out = [
        pltpu.make_async_copy(cut(held[i], k), cut(targets[i], k), out_sem.at[i, k])
        for i, k in pieces
    ]
    for copy in into:
        copy.start()
    for first, second in zip(into, out):
        first.wait()
        second.start()
    for copy in out:
        copy.wait()


def per_device(count, *args):
    u, v, t, spin, thick, visc, depth, sea, wet = args
    levels, rows, columns = u.shape
    half = rows // 2
    span = half + 2 * HALO
    assert rows == TS and columns == 2 * TS
    peers = 2 * count
    f32 = jnp.float32
    anywhere = pl.BlockSpec(memory_space=pl.ANY)
    vmem = pl.BlockSpec(memory_space=pltpu.VMEM)
    smem = pl.BlockSpec(memory_space=pltpu.SMEM)
    dma = pltpu.SemaphoreType.DMA
    fields = pl.pallas_call(
        functools.partial(kernel, count),
        out_shape=[jax.ShapeDtypeStruct(u.shape, f32)] * 3
        + [jax.ShapeDtypeStruct(sea.shape, f32)] * 2,
        in_specs=[anywhere, anywhere, anywhere, vmem, smem, anywhere, anywhere, anywhere, smem],
        out_specs=[anywhere] * 5,
        scratch_shapes=[
            pltpu.VMEM((rows, columns), f32),
            pltpu.VMEM((2, 3, levels, span, columns), f32),
            pltpu.VMEM((2, 4, span, columns), f32),
            pltpu.VMEM((2, 3, levels, half, columns), f32),
            pltpu.VMEM((2, 2, half, columns), f32),
            pltpu.VMEM((2, 13, span, columns), f32),
            pltpu.VMEM((2, 4, span, columns), f32),
            pltpu.VMEM((peers, 16, columns), f32),
            dma((3, CHUNKS + 1)),
            dma((3, CHUNKS + 1)),
            dma((3, CHUNKS + 1)),
            dma((2, 4, CHUNKS + 1)),
            dma((2, 4, CHUNKS + 1)),
            dma((3, CHUNKS + 1)),
            dma((3, CHUNKS + 1)),
            dma((3, CHUNKS + 1)),
            dma((peers,)),
            dma((peers,)),
        ],
        compiler_params=pltpu.CompilerParams(
            collective_id=0, has_side_effects=True, vmem_limit_bytes=VMEM_BYTES
        ),
    )(u, v, t, spin.reshape(1, rows), thick, visc, depth, sea, wet.T)
    return pl.pallas_call(
        deliver,
        out_shape=[jax.ShapeDtypeStruct(a.shape, f32) for a in fields],
        in_specs=[anywhere] * 5,
        out_specs=[anywhere] * 5,
        scratch_shapes=[pltpu.VMEM(a.shape, f32) for a in fields]
        + [dma((5, CHUNKS)), dma((5, CHUNKS))],
        compiler_params=pltpu.CompilerParams(vmem_limit_bytes=VMEM_BYTES),
    )(*fields)


def solution(mesh):
    cells = P(None, ("group", "gx"), "gy")
    flat = P(("group", "gx"), "gy")
    assert mesh.shape["gy"] == 2
    return jax.shard_map(
        functools.partial(per_device, mesh.shape["gx"]),
        mesh=mesh,
        in_specs=(cells, cells, cells, P("gx"), P(), P("gx", "gy"), P("gx", "gy"), flat, P()),
        out_specs=(cells, cells, cells, flat, flat),
        check_vma=False,
    )
```

```python
import functools

import jax
import jax.numpy as jnp
from jax import lax
from jax.experimental import pallas as pl
from jax.experimental.pallas import tpu as pltpu
from jax.sharding import PartitionSpec as P

TS = 64
ITERS = 3
CHUNKS = 4
HALO = 8
VMEM_BYTES = 60 * 1024 * 1024

pressure_coef = 0.02
biharmonic_coef = 0.02
advection_coef = 0.5
surface_coef = 0.5
divergence_coef = 0.1

MESH = pl.DeviceIdType.MESH


def kernel(
    count,
    u_ref, v_ref, t_ref, spin_ref, thick_ref, visc_ref, depth_ref, sea_ref, wet_ref,
    ou_ref, ov_ref, ot_ref, ox_ref, or_ref,
    own, own_flat, buf, buf2, res, res2, weights, total, krylov, gathered, own_sem,
    local_sem, swap_send, swap_recv, halo_send, halo_recv,
    out_sem, back_send, back_recv, gram_send, gram_recv,
):
    levels, rows, columns = u_ref.shape
    half = rows // 2
    span = half + 2 * HALO
    reach = half + HALO
    per = levels // CHUNKS
    group = lax.axis_index("group")
    gx = lax.axis_index("gx")
    core = lax.axis_index("gy")
    other = 1 - core
    peers = 2 * count
    me = gx * 2 + core

    barrier = pltpu.get_barrier_semaphore()

    def greet(k, _):
        peer = lax.rem(me + k, peers)
        pl.semaphore_signal(
            barrier, inc=1, device_id=(group, peer // 2, lax.rem(peer, 2)), device_id_type=MESH
        )
        return 0

    lax.fori_loop(1, peers, greet, 0)

    own_loads = [
        pltpu.make_async_copy(ref, own.at[f], own_sem.at[f])
        for f, ref in enumerate((u_ref, v_ref, t_ref))
    ]
    for copy in own_loads:
        copy.start()

    spin_row = jnp.broadcast_to(spin_ref[...], (rows, rows))
    diagonal = lax.broadcasted_iota(jnp.int32, (rows, rows), 0) == lax.broadcasted_iota(
        jnp.int32, (rows, rows), 1
    )
    spin_column = jnp.sum(jnp.where(diagonal, spin_row, 0.0), axis=1, keepdims=True)
    own_flat[0] = jnp.broadcast_to(spin_column, (rows, columns))

    def taken(c):
        return pl.ds(pl.multiple_of((half - HALO) * c, 8), reach)

    def placed(c):
        return pl.ds(pl.multiple_of(HALO - HALO * c, 8), reach)

    has_outer = jnp.where(core == 0, gx > 0, gx < count - 1)
    cells = (u_ref, v_ref, t_ref)
    flats = (visc_ref, depth_ref, sea_ref) + tuple(own_flat.at[i] for i in range(4))
    swapped = (0, 1, 2, 4, 5, 6)

    def source(f, k, where):
        if k is None:
            return flats[f].at[where, :]
        return cells[f].at[pl.ds(k * per, per), where, :]

    def target(f, k, which, where):
        if k is None:
            return buf2.at[which, f, where, :]
        return buf.at[which, f, pl.ds(k * per, per), where, :]

    def slot(k):
        return CHUNKS if k is None else k

    def swap(f, k):
        return pltpu.make_async_remote_copy(
            src_ref=source(f, k, taken(other)),
            dst_ref=target(f, k, core, placed(other)),
            send_sem=swap_send.at[f, slot(k)],
            recv_sem=swap_recv.at[f, slot(k)],
            device_id=(group, gx, other),
            device_id_type=MESH,
        )

    def keep(f, k):
        return pltpu.make_async_copy(
            source(f, k, taken(core)),
            target(f, k, core, placed(core)),
            local_sem.at[f, slot(k)],
        )

    def halo_down(f, k):
        return pltpu.make_async_remote_copy(
            src_ref=source(f, k, pl.ds(rows - HALO, HALO)),
            dst_ref=target(f, k, core, pl.ds(0, HALO)),
            send_sem=halo_send.at[0, f, slot(k)],
            recv_sem=halo_recv.at[core, f, slot(k)],
            device_id=(group, lax.rem(gx + 1, count), 0),
            device_id_type=MESH,
        )

    def halo_up(f, k):
        return pltpu.make_async_remote_copy(
            src_ref=source(f, k, pl.ds(0, HALO)),
            dst_ref=target(f, k, core, pl.ds(HALO + half, HALO)),
            send_sem=halo_send.at[1, f, slot(k)],
            recv_sem=halo_recv.at[core, f, slot(k)],
            device_id=(group, lax.rem(gx + count - 1, count), 1),
            device_id_type=MESH,
        )

    def halo_in(f, k, h):
        return pltpu.make_async_remote_copy(
            src_ref=source(f, k, pl.ds(0, HALO)),
            dst_ref=target(f, k, h, pl.ds(0, HALO)),
            send_sem=halo_send.at[0, f, slot(k)],
            recv_sem=halo_recv.at[h, f, slot(k)],
            device_id=(group, gx, other),
            device_id_type=MESH,
        )

    def span_of(k):
        return range(7) if k is None else range(3)

    def send_halo(k):
        @pl.when(gx < count - 1)
        def _():
            for f in span_of(k):
                halo_down(f, k).start()

        @pl.when(gx > 0)
        def _():
            for f in span_of(k):
                halo_up(f, k).start()

    def send_swap(k):
        for f in swapped if k is None else range(3):
            swap(f, k).start()

    def arrive(k):
        for f in range(3):
            keep(f, k).wait()
        for f in swapped if k is None else range(3):
            swap(f, k).wait_recv()

        @pl.when(has_outer)
        def _():
            for f in span_of(k):
                halo_in(f, k, 0).wait_recv()
                halo_in(f, k, 1).wait_recv()

    def sent(k):
        for f in swapped if k is None else range(3):
            swap(f, k).wait_send()

        @pl.when(gx < count - 1)
        def _():
            for f in span_of(k):
                halo_down(f, k).wait_send()

        @pl.when(gx > 0)
        def _():
            for f in span_of(k):
                halo_up(f, k).wait_send()

    everything = [None] + list(range(CHUNKS))
    for k in everything:
        for f in range(3):
            keep(f, k).start()
    own_rows = own_flat[0, taken(core), :]
    for h in range(2):
        buf2[h, 3, placed(core), :] = own_rows
    for copy in own_loads:
        copy.wait()

    nothing = jnp.zeros((rows, columns), jnp.float32)
    for i in range(1, 4):
        own_flat[i] = nothing

    def integrate(l, heat):
        thickness = thick_ref[l]
        column = thickness * own[2, l]
        heat = heat + column
        own_flat[1] += thickness * own[0, l]
        own_flat[2] += thickness * own[1, l]
        own_flat[3] += thickness * (heat - 0.5 * column)
        return heat

    lax.fori_loop(0, levels, integrate, nothing)
    for i in range(1, 4):
        buf2[core, 3 + i, placed(core), :] = own_flat[i, taken(core), :]
    first = gx == 0
    last = gx == count - 1

    def clear(start):
        def one(l, _):
            for h in range(2):
                for f in range(3):
                    buf[h, f, l, start : start + HALO, :] = jnp.zeros((HALO, columns), jnp.float32)
            return 0

        lax.fori_loop(0, levels, one, 0)
        for h in range(2):
            for f in range(7):
                buf2[h, f, start : start + HALO, :] = jnp.zeros((HALO, columns), jnp.float32)

    @pl.when(jnp.logical_and(first, core == 0))
    def _():
        clear(0)

    @pl.when(jnp.logical_and(last, core == 1))
    def _():
        clear(HALO + half)

    pl.semaphore_wait(barrier, peers - 1)
    for k in everything:
        send_halo(k)
        send_swap(k)

    lane = lax.broadcasted_iota(jnp.int32, (span, columns), 1)
    row = lax.broadcasted_iota(jnp.int32, (span, columns), 0)
    at_left = lane == 0
    at_right = lane == columns - 1

    def up(a):
        return pltpu.roll(a, 1, 0)

    def down(a):
        return pltpu.roll(a, span - 1, 0)

    def left(pair):
        r0, r1 = [pltpu.roll(a, 1, 1) for a in pair]
        return [jnp.where(at_left, 0.0, r0), jnp.where(at_left, r0, r1)]

    def right(pair):
        r0, r1 = [pltpu.roll(a, columns - 1, 1) for a in pair]
        return [jnp.where(at_right, r1, r0), jnp.where(at_right, 0.0, r1)]

    def around(pair):
        return [up(a) for a in pair], [down(a) for a in pair], left(pair), right(pair)

    outer_tile = jnp.where(core == 0, gx - 1, gx + 1)
    outer_tile_safe = jnp.clip(outer_tile, 0, count - 1)
    outer_flag = jnp.where(has_outer, 1, 0)
    in_outer = jnp.where(core == 0, row, span - 1 - row) < HALO
    mask = []
    for h in range(2):
        inner = jnp.where(lane < TS, wet_ref[2 * h, gx], wet_ref[2 * h + 1, gx])
        outer = jnp.where(
            lane < TS,
            wet_ref[2 * h, outer_tile_safe] * outer_flag,
            wet_ref[2 * h + 1, outer_tile_safe] * outer_flag,
        )
        mask.append(jnp.where(in_outer, outer, inner).astype(jnp.float32))
    sides = around(mask)
    for h in range(2):
        m = mask[h]
        mu, md, ml, mr = [side[h] for side in sides]
        number = mu + md + ml + mr
        weights[h, 0] = m
        weights[h, 1] = number
        weights[h, 2] = mu
        weights[h, 3] = md
        weights[h, 4] = ml
        weights[h, 5] = mr
        weights[h, 6] = mu - md
        weights[h, 7] = ml - mr

    arrive(None)

    def face_weights(pair):
        ring = around(pair)
        result = []
        for h in range(2):
            four = [
                0.5 * (pair[h] + ring[side][h]) * mask[h] * sides[side][h] for side in range(4)
            ]
            result.append(four)
        return result

    viscous = face_weights([buf2[0, 0], buf2[1, 0]])
    for h in range(2):
        for side in range(4):
            weights[h, 8 + side] = viscous[h][side]
        weights[h, 12] = viscous[h][0] + viscous[h][1] + viscous[h][2] + viscous[h][3]

    face = face_weights([buf2[0, 1], buf2[1, 1]])
    scaling = [
        surface_coef + (face[h][0] + face[h][1]) + (face[h][2] + face[h][3]) for h in range(2)
    ]
    inverse = [1.0 / scaling[h] for h in range(2)]
    flat = [[buf2[h, f] * mask[h] for h in range(2)] for f in range(4, 7)]
    rings = [around(pair) for pair in flat]
    unit = [sides[0][h] + sides[1][h] + sides[2][h] + sides[3][h] for h in range(2)]
    flow = []
    for f in range(2):
        once = [
            mask[h]
            * (
                (rings[f][0][h] + rings[f][1][h])
                + (rings[f][2][h] + rings[f][3][h])
                - unit[h] * flat[f][h]
            )
            for h in range(2)
        ]
        ring = around(once)
        sign = 1.0 - 2.0 * f
        total_flow = []
        for h in range(2):
            if f == 0:
                slope = rings[2][1][h] - rings[2][0][h] + weights[h, 6] * flat[2][h]
            else:
                slope = rings[2][3][h] - rings[2][2][h] + weights[h, 7] * flat[2][h]
            smooth = (
                weights[h, 8] * rings[f][0][h]
                + weights[h, 9] * rings[f][1][h]
                + (weights[h, 10] * rings[f][2][h] + weights[h, 11] * rings[f][3][h])
                - weights[h, 12] * flat[f][h]
            )
            twice = (ring[0][h] + ring[1][h]) + (ring[2][h] + ring[3][h]) - unit[h] * once[h]
            total_flow.append(
                mask[h]
                * (
                    flat[f][h]
                    + sign * buf2[h, 3] * flat[1 - f][h]
                    - (0.5 * pressure_coef) * slope
                    + smooth
                    - biharmonic_coef * twice
                )
            )
        flow.append(total_flow)
    flow_u, flow_v = flow
    before, after = left(flow_v), right(flow_v)
    vectors = [
        [
            mask[h]
            * (
                surface_coef * buf2[h, 2]
                - (0.5 * divergence_coef)
                * ((down(flow_u[h]) - up(flow_u[h])) + (after[h] - before[h]))
            )
            * inverse[h]
            for h in range(2)
        ]
    ]
    for _ in range(ITERS):
        ring = around(vectors[-1])
        vectors.append(
            [
                (
                    (face[h][0] * ring[0][h] + face[h][1] * ring[1][h])
                    + (face[h][2] * ring[2][h] + face[h][3] * ring[3][h])
                )
                * inverse[h]
                for h in range(2)
            ]
        )
    inside = slice(HALO, HALO + half)
    basis = [[pair[h][inside] for h in range(2)] for pair in vectors]
    scale = [scaling[h][inside] for h in range(2)]

    def dot(a, b):
        both = scale[0] * a[0] * b[0] + scale[1] * a[1] * b[1]
        return jnp.sum(both, axis=0, keepdims=True)

    moments = 2 * ITERS - 1
    difference = [
        [basis[k][h] - basis[k + 1][h] for h in range(2)] for k in range(ITERS)
    ]
    gathered[me] = jnp.zeros(gathered.shape[1:], jnp.float32)
    lines = [dot(basis[(k + 1) // 2], basis[k // 2]) for k in range(moments)]
    lines += [dot(basis[(k + 1) // 2], difference[k // 2]) for k in range(moments)]
    for k, line in enumerate(lines):
        gathered[me, k : k + 1, :] = line

    def gram(k):
        peer = lax.rem(me + k, peers)
        return pltpu.make_async_remote_copy(
            src_ref=gathered.at[me],
            dst_ref=gathered.at[me],
            send_sem=gram_send.at[k],
            recv_sem=gram_recv.at[me],
            device_id=(group, peer // 2, lax.rem(peer, 2)),
            device_id_type=MESH,
        )

    def gram_from(k):
        peer = lax.rem(me + k, peers)
        return pltpu.make_async_remote_copy(
            src_ref=gathered.at[peer],
            dst_ref=gathered.at[peer],
            send_sem=gram_send.at[k],
            recv_sem=gram_recv.at[peer],
            device_id=(group, peer // 2, lax.rem(peer, 2)),
            device_id_type=MESH,
        )

    def gram_start(k, _):
        gram(k).start()
        return 0

    def gram_wait(k, _):
        gram_from(k).wait_recv()
        return 0

    def gram_sent(k, _):
        gram(k).wait_send()
        return 0

    lax.fori_loop(1, peers, gram_start, 0)
    for h in range(2):
        for j in range(ITERS + 1):
            krylov[h, j] = basis[j][h]
        krylov[h, ITERS + 1] = scale[h]

    for h in range(2):
        for i in range(4):
            total[h, i] = jnp.zeros((span, columns), jnp.float32)

    def level(l, _):
        thickness = thick_ref[l]
        fields = []
        rings = []
        for f in range(3):
            pair = [buf[h, f, l] * weights[h, 0] for h in range(2)]
            fields.append(pair)
            rings.append(around(pair))
        u, v, t = fields
        viscous_part = []
        for f in range(3):
            viscous_part.append(
                [
                    weights[h, 8] * rings[f][0][h]
                    + weights[h, 9] * rings[f][1][h]
                    + (weights[h, 10] * rings[f][2][h] + weights[h, 11] * rings[f][3][h])
                    - weights[h, 12] * fields[f][h]
                    for h in range(2)
                ]
            )
        hyper = []
        for f in range(2):
            once = [
                weights[h, 0]
                * (
                    (rings[f][0][h] + rings[f][1][h])
                    + (rings[f][2][h] + rings[f][3][h])
                    - weights[h, 1] * fields[f][h]
                )
                for h in range(2)
            ]
            ring = around(once)
            hyper.append(
                [
                    (ring[0][h] + ring[1][h]) + (ring[2][h] + ring[3][h]) - weights[h, 1] * once[h]
                    for h in range(2)
                ]
            )
        tu, td, tl, tr = rings[2]
        uu, ud, _, _ = rings[0]
        _, _, vl, vr = rings[1]
        for h in range(2):
            m = weights[h, 0]
            slope_row = thickness * (td[h] - tu[h] + weights[h, 6] * t[h])
            slope_column = thickness * (tr[h] - tl[h] + weights[h, 7] * t[h])
            sum_row = total[h, 2] + slope_row
            sum_column = total[h, 3] + slope_column
            total[h, 2] = sum_row
            total[h, 3] = sum_column
            grad_row = sum_row - 0.5 * slope_row
            grad_column = sum_column - 0.5 * slope_column
            spread = (
                weights[h, 3] * ((u[h] + ud[h]) * (t[h] + td[h]))
                - weights[h, 2] * ((u[h] + uu[h]) * (t[h] + tu[h]))
                + (
                    weights[h, 5] * ((v[h] + vr[h]) * (t[h] + tr[h]))
                    - weights[h, 4] * ((v[h] + vl[h]) * (t[h] + tl[h]))
                )
            )
            spin = buf2[h, 3]
            u_next = m * (
                u[h]
                + spin * v[h]
                - (0.5 * pressure_coef) * grad_row
                + viscous_part[0][h]
                - biharmonic_coef * hyper[0][h]
            )
            v_next = m * (
                v[h]
                - spin * u[h]
                - (0.5 * pressure_coef) * grad_column
                + viscous_part[1][h]
                - biharmonic_coef * hyper[1][h]
            )
            t_next = m * (t[h] - (0.25 * advection_coef) * spread + viscous_part[2][h])
            res[h, 0, l] = u_next[HALO : HALO + half]
            res[h, 1, l] = v_next[HALO : HALO + half]
            res[h, 2, l] = t_next[HALO : HALO + half]
        return 0

    mine = pl.ds(pl.multiple_of(half * core, 8), half)

    def outs(k):
        part = pl.ds(k * per, per)
        local = [
            pltpu.make_async_copy(
                res.at[core, f, part], ref.at[part, mine, :], out_sem.at[f, k]
            )
            for f, ref in enumerate((ou_ref, ov_ref, ot_ref))
        ]
        remote = [
            pltpu.make_async_remote_copy(
                src_ref=res.at[other, f, part],
                dst_ref=ref.at[part, mine, :],
                send_sem=back_send.at[f, k],
                recv_sem=back_recv.at[f, k],
                device_id=(group, gx, other),
                device_id_type=MESH,
            )
            for f, ref in enumerate((ou_ref, ov_ref, ot_ref))
        ]
        return remote + local

    def chunk(k, _):
        arrive(k)
        lax.fori_loop(k * per, (k + 1) * per, level, 0)
        for copy in outs(k):
            copy.start()
        return 0

    lax.fori_loop(0, CHUNKS, chunk, 0)

    lax.fori_loop(1, peers, gram_wait, 0)

    summed = lax.fori_loop(
        0, peers, lambda k, acc: acc + gathered[k], jnp.zeros(gathered.shape[1:], jnp.float32)
    )
    sums = jnp.sum(summed, axis=1, keepdims=True)
    mass = [sums[k : k + 1] for k in range(moments)]
    stiff = [sums[moments + k : moments + k + 1] for k in range(moments)]

    def quadratic(coefs, table):
        value = None
        for i, a in enumerate(coefs):
            for j, b in enumerate(coefs):
                term = a * b * table[i + j]
                value = term if value is None else value + term
        return value

    one = jnp.ones((1, 1), jnp.float32)
    zero = jnp.zeros((1, 1), jnp.float32)
    remains = [one]
    heading = [one]
    guess = [zero] * ITERS
    rho = mass[0]
    for iteration in range(ITERS):
        step = rho / quadratic(heading, stiff)
        for j, c in enumerate(heading):
            guess[j] = guess[j] + step * c
        moved = remains + [zero]
        for j, c in enumerate(heading):
            moved[j] = moved[j] - step * c
            moved[j + 1] = moved[j + 1] + step * c
        remains = moved
        if iteration + 1 < ITERS:
            rho_new = quadratic(remains, mass)
            ratio = rho_new / rho
            heading = [
                remains[j] + ratio * heading[j] if j < len(heading) else remains[j]
                for j in range(len(remains))
            ]
            rho = rho_new

    for h in range(2):
        x = guess[0] * krylov[h, 0]
        for j in range(1, ITERS):
            x = x + guess[j] * krylov[h, j]
        r = remains[0] * krylov[h, 0]
        for j in range(1, ITERS + 1):
            r = r + remains[j] * krylov[h, j]
        res2[h, 0] = x
        res2[h, 1] = krylov[h, ITERS + 1] * r

    def flat_outs():
        k = CHUNKS
        local = [
            pltpu.make_async_copy(res2.at[core, f], ref.at[mine, :], out_sem.at[f, k])
            for f, ref in enumerate((ox_ref, or_ref))
        ]
        remote = [
            pltpu.make_async_remote_copy(
                src_ref=res2.at[other, f],
                dst_ref=ref.at[mine, :],
                send_sem=back_send.at[f, k],
                recv_sem=back_recv.at[f, k],
                device_id=(group, gx, other),
                device_id_type=MESH,
            )
            for f, ref in enumerate((ox_ref, or_ref))
        ]
        return remote + local

    for copy in flat_outs():
        copy.start()
    lax.fori_loop(1, peers, gram_sent, 0)
    sent(None)
    for k in range(CHUNKS):
        sent(k)
        for copy in outs(k):
            copy.wait()
    for copy in flat_outs():
        copy.wait()


def deliver(*refs):
    sources, targets, held = refs[:5], refs[5:10], refs[10:15]
    into_sem, out_sem = refs[15:]

    def cut(ref, k):
        size = ref.shape[0] // CHUNKS
        return ref.at[pl.ds(k * size, size)]

    pieces = [(i, k) for k in range(CHUNKS) for i in range(5)]
    into = [
        pltpu.make_async_copy(cut(sources[i], k), cut(held[i], k), into_sem.at[i, k])
        for i, k in pieces
    ]
    out = [
        pltpu.make_async_copy(cut(held[i], k), cut(targets[i], k), out_sem.at[i, k])
        for i, k in pieces
    ]
    for copy in into:
        copy.start()
    for first, second in zip(into, out):
        first.wait()
        second.start()
    for copy in out:
        copy.wait()


def per_device(count, *args):
    u, v, t, spin, thick, visc, depth, sea, wet = args
    levels, rows, columns = u.shape
    half = rows // 2
    span = half + 2 * HALO
    assert rows == TS and columns == 2 * TS
    peers = 2 * count
    f32 = jnp.float32
    anywhere = pl.BlockSpec(memory_space=pl.ANY)
    vmem = pl.BlockSpec(memory_space=pltpu.VMEM)
    smem = pl.BlockSpec(memory_space=pltpu.SMEM)
    dma = pltpu.SemaphoreType.DMA
    fields = pl.pallas_call(
        functools.partial(kernel, count),
        out_shape=[jax.ShapeDtypeStruct(u.shape, f32)] * 3
        + [jax.ShapeDtypeStruct(sea.shape, f32)] * 2,
        in_specs=[anywhere, anywhere, anywhere, vmem, smem, anywhere, anywhere, anywhere, smem],
        out_specs=[anywhere] * 5,
        scratch_shapes=[
            pltpu.VMEM((3, levels, rows, columns), f32),
            pltpu.VMEM((4, rows, columns), f32),
            pltpu.VMEM((2, 3, levels, span, columns), f32),
            pltpu.VMEM((2, 7, span, columns), f32),
            pltpu.VMEM((2, 3, levels, half, columns), f32),
            pltpu.VMEM((2, 2, half, columns), f32),
            pltpu.VMEM((2, 13, span, columns), f32),
            pltpu.VMEM((2, 4, span, columns), f32),
            pltpu.VMEM((2, ITERS + 2, half, columns), f32),
            pltpu.VMEM((peers, 16, columns), f32),
            dma((3,)),
            dma((3, CHUNKS + 1)),
            dma((7, CHUNKS + 1)),
            dma((7, CHUNKS + 1)),
            dma((2, 7, CHUNKS + 1)),
            dma((2, 7, CHUNKS + 1)),
            dma((3, CHUNKS + 1)),
            dma((3, CHUNKS + 1)),
            dma((3, CHUNKS + 1)),
            dma((peers,)),
            dma((peers,)),
        ],
        compiler_params=pltpu.CompilerParams(
            collective_id=0, has_side_effects=True, vmem_limit_bytes=VMEM_BYTES
        ),
    )(u, v, t, spin.reshape(1, rows), thick, visc, depth, sea, wet.T)
    return pl.pallas_call(
        deliver,
        out_shape=[jax.ShapeDtypeStruct(a.shape, f32) for a in fields],
        in_specs=[anywhere] * 5,
        out_specs=[anywhere] * 5,
        scratch_shapes=[pltpu.VMEM(a.shape, f32) for a in fields]
        + [dma((5, CHUNKS)), dma((5, CHUNKS))],
        compiler_params=pltpu.CompilerParams(vmem_limit_bytes=VMEM_BYTES),
    )(*fields)


def solution(mesh):
    cells = P(None, ("group", "gx"), "gy")
    flat = P(("group", "gx"), "gy")
    assert mesh.shape["gy"] == 2
    return jax.shard_map(
        functools.partial(per_device, mesh.shape["gx"]),
        mesh=mesh,
        in_specs=(cells, cells, cells, P("gx"), P(), P("gx", "gy"), P("gx", "gy"), flat, P()),
        out_specs=(cells, cells, cells, flat, flat),
        check_vma=False,
    )
```

```python
import functools

import jax
import jax.numpy as jnp
from jax import lax
from jax.experimental import pallas as pl
from jax.experimental.pallas import tpu as pltpu
from jax.sharding import PartitionSpec as P

TS = 64
ITERS = 3
CHUNKS = 4
HALO = 8
NEAR = 2
VMEM_BYTES = 60 * 1024 * 1024

pressure_coef = 0.02
biharmonic_coef = 0.02
advection_coef = 0.5
surface_coef = 0.5
divergence_coef = 0.1

MESH = pl.DeviceIdType.MESH


def kernel(
    count,
    u_ref, v_ref, t_ref, spin_ref, thick_ref, visc_ref, depth_ref, sea_ref, wet_ref,
    ou_ref, ov_ref, ot_ref, ox_ref, or_ref,
    own, own_flat, buf, buf2, res, res2, weights, total, krylov, gathered, own_sem,
    local_sem, swap_send, swap_recv, halo_send, halo_recv,
    out_sem, back_send, back_recv, gram_send, gram_recv,
):
    levels, rows, columns = u_ref.shape
    half = rows // 2
    span = half + 2 * HALO
    reach = half + HALO
    per = levels // CHUNKS
    group = lax.axis_index("group")
    gx = lax.axis_index("gx")
    core = lax.axis_index("gy")
    other = 1 - core
    peers = 2 * count
    me = gx * 2 + core

    barrier = pltpu.get_barrier_semaphore()

    def greet(k, _):
        peer = lax.rem(me + k, peers)
        pl.semaphore_signal(
            barrier, inc=1, device_id=(group, peer // 2, lax.rem(peer, 2)), device_id_type=MESH
        )
        return 0

    lax.fori_loop(1, peers, greet, 0)

    own_loads = [
        pltpu.make_async_copy(ref, own.at[f], own_sem.at[f])
        for f, ref in enumerate((u_ref, v_ref, t_ref))
    ]
    for copy in own_loads:
        copy.start()

    spin_row = jnp.broadcast_to(spin_ref[...], (rows, rows))
    diagonal = lax.broadcasted_iota(jnp.int32, (rows, rows), 0) == lax.broadcasted_iota(
        jnp.int32, (rows, rows), 1
    )
    spin_column = jnp.sum(jnp.where(diagonal, spin_row, 0.0), axis=1, keepdims=True)
    own_flat[0] = jnp.broadcast_to(spin_column, (rows, columns))

    def taken(c):
        return pl.ds(pl.multiple_of((half - HALO) * c, 8), reach)

    def placed(c):
        return pl.ds(pl.multiple_of(HALO - HALO * c, 8), reach)

    has_outer = jnp.where(core == 0, gx > 0, gx < count - 1)
    cells = (u_ref, v_ref, t_ref)
    flats = (visc_ref, depth_ref, sea_ref) + tuple(own_flat.at[i] for i in range(4))
    swapped = (0, 1, 2, 4, 5, 6)

    def source(f, k, where):
        if k is None:
            return flats[f].at[where, :]
        return cells[f].at[pl.ds(k * per, per), where, :]

    def target(f, k, which, where):
        if k is None:
            return buf2.at[which, f, where, :]
        return buf.at[which, f, pl.ds(k * per, per), where, :]

    def slot(k):
        return CHUNKS if k is None else k

    def swap(f, k):
        return pltpu.make_async_remote_copy(
            src_ref=source(f, k, taken(other)),
            dst_ref=target(f, k, core, placed(other)),
            send_sem=swap_send.at[f, slot(k)],
            recv_sem=swap_recv.at[f, slot(k)],
            device_id=(group, gx, other),
            device_id_type=MESH,
        )

    def keep(f, k):
        return pltpu.make_async_copy(
            source(f, k, taken(core)),
            target(f, k, core, placed(core)),
            local_sem.at[f, slot(k)],
        )

    def depth_of(k):
        return HALO if k is None else NEAR

    def halo_down(f, k):
        return pltpu.make_async_remote_copy(
            src_ref=source(f, k, pl.ds(rows - depth_of(k), depth_of(k))),
            dst_ref=target(f, k, core, pl.ds(HALO - depth_of(k), depth_of(k))),
            send_sem=halo_send.at[0, f, slot(k)],
            recv_sem=halo_recv.at[core, f, slot(k)],
            device_id=(group, lax.rem(gx + 1, count), 0),
            device_id_type=MESH,
        )

    def halo_up(f, k):
        return pltpu.make_async_remote_copy(
            src_ref=source(f, k, pl.ds(0, depth_of(k))),
            dst_ref=target(f, k, core, pl.ds(HALO + half, depth_of(k))),
            send_sem=halo_send.at[1, f, slot(k)],
            recv_sem=halo_recv.at[core, f, slot(k)],
            device_id=(group, lax.rem(gx + count - 1, count), 1),
            device_id_type=MESH,
        )

    def halo_in(f, k, h):
        return pltpu.make_async_remote_copy(
            src_ref=source(f, k, pl.ds(0, depth_of(k))),
            dst_ref=target(f, k, h, pl.ds(HALO - depth_of(k), depth_of(k))),
            send_sem=halo_send.at[0, f, slot(k)],
            recv_sem=halo_recv.at[h, f, slot(k)],
            device_id=(group, gx, other),
            device_id_type=MESH,
        )

    def span_of(k):
        return range(7) if k is None else range(3)

    def send_halo(k):
        @pl.when(gx < count - 1)
        def _():
            for f in span_of(k):
                halo_down(f, k).start()

        @pl.when(gx > 0)
        def _():
            for f in span_of(k):
                halo_up(f, k).start()

    def send_swap(k):
        for f in swapped if k is None else range(3):
            swap(f, k).start()

    def arrive(k):
        for f in range(3):
            keep(f, k).wait()
        for f in swapped if k is None else range(3):
            swap(f, k).wait_recv()

        @pl.when(has_outer)
        def _():
            for f in span_of(k):
                halo_in(f, k, 0).wait_recv()
                halo_in(f, k, 1).wait_recv()

    def sent(k):
        for f in swapped if k is None else range(3):
            swap(f, k).wait_send()

        @pl.when(gx < count - 1)
        def _():
            for f in span_of(k):
                halo_down(f, k).wait_send()

        @pl.when(gx > 0)
        def _():
            for f in span_of(k):
                halo_up(f, k).wait_send()

    everything = [None] + list(range(CHUNKS))
    for k in everything:
        for f in range(3):
            keep(f, k).start()
    own_rows = own_flat[0, taken(core), :]
    for h in range(2):
        buf2[h, 3, placed(core), :] = own_rows
    for copy in own_loads:
        copy.wait()

    nothing = jnp.zeros((rows, columns), jnp.float32)
    for i in range(1, 4):
        own_flat[i] = nothing

    def integrate(l, heat):
        thickness = thick_ref[l]
        column = thickness * own[2, l]
        heat = heat + column
        own_flat[1] += thickness * own[0, l]
        own_flat[2] += thickness * own[1, l]
        own_flat[3] += thickness * (heat - 0.5 * column)
        return heat

    lax.fori_loop(0, levels, integrate, nothing)
    for i in range(1, 4):
        buf2[core, 3 + i, placed(core), :] = own_flat[i, taken(core), :]
    first = gx == 0
    last = gx == count - 1

    def clear(start):
        def one(l, _):
            for h in range(2):
                for f in range(3):
                    buf[h, f, l, start : start + HALO, :] = jnp.zeros((HALO, columns), jnp.float32)
            return 0

        lax.fori_loop(0, levels, one, 0)
        for h in range(2):
            for f in range(7):
                buf2[h, f, start : start + HALO, :] = jnp.zeros((HALO, columns), jnp.float32)

    @pl.when(jnp.logical_and(first, core == 0))
    def _():
        clear(0)

    @pl.when(jnp.logical_and(last, core == 1))
    def _():
        clear(HALO + half)

    pl.semaphore_wait(barrier, peers - 1)
    for k in everything:
        send_halo(k)
        send_swap(k)

    lane = lax.broadcasted_iota(jnp.int32, (span, columns), 1)
    row = lax.broadcasted_iota(jnp.int32, (span, columns), 0)
    at_left = lane == 0
    at_right = lane == columns - 1

    def up(a):
        return pltpu.roll(a, 1, 0)

    def down(a):
        return pltpu.roll(a, span - 1, 0)

    def left(pair):
        r0, r1 = [pltpu.roll(a, 1, 1) for a in pair]
        return [jnp.where(at_left, 0.0, r0), jnp.where(at_left, r0, r1)]

    def right(pair):
        r0, r1 = [pltpu.roll(a, columns - 1, 1) for a in pair]
        return [jnp.where(at_right, r1, r0), jnp.where(at_right, 0.0, r1)]

    def around(pair):
        return [up(a) for a in pair], [down(a) for a in pair], left(pair), right(pair)

    outer_tile = jnp.where(core == 0, gx - 1, gx + 1)
    outer_tile_safe = jnp.clip(outer_tile, 0, count - 1)
    outer_flag = jnp.where(has_outer, 1, 0)
    in_outer = jnp.where(core == 0, row, span - 1 - row) < HALO
    mask = []
    for h in range(2):
        inner = jnp.where(lane < TS, wet_ref[2 * h, gx], wet_ref[2 * h + 1, gx])
        outer = jnp.where(
            lane < TS,
            wet_ref[2 * h, outer_tile_safe] * outer_flag,
            wet_ref[2 * h + 1, outer_tile_safe] * outer_flag,
        )
        mask.append(jnp.where(in_outer, outer, inner).astype(jnp.float32))
    sides = around(mask)
    for h in range(2):
        m = mask[h]
        mu, md, ml, mr = [side[h] for side in sides]
        number = mu + md + ml + mr
        weights[h, 0] = m
        weights[h, 1] = number
        weights[h, 2] = mu
        weights[h, 3] = md
        weights[h, 4] = ml
        weights[h, 5] = mr
        weights[h, 6] = mu - md
        weights[h, 7] = ml - mr

    arrive(None)

    def face_weights(pair):
        ring = around(pair)
        result = []
        for h in range(2):
            four = [
                0.5 * (pair[h] + ring[side][h]) * mask[h] * sides[side][h] for side in range(4)
            ]
            result.append(four)
        return result

    viscous = face_weights([buf2[0, 0], buf2[1, 0]])
    for h in range(2):
        for side in range(4):
            weights[h, 8 + side] = viscous[h][side]
        weights[h, 12] = viscous[h][0] + viscous[h][1] + viscous[h][2] + viscous[h][3]

    face = face_weights([buf2[0, 1], buf2[1, 1]])
    scaling = [
        surface_coef + (face[h][0] + face[h][1]) + (face[h][2] + face[h][3]) for h in range(2)
    ]
    inverse = [1.0 / scaling[h] for h in range(2)]
    flat = [[buf2[h, f] * mask[h] for h in range(2)] for f in range(4, 7)]
    rings = [around(pair) for pair in flat]
    unit = [sides[0][h] + sides[1][h] + sides[2][h] + sides[3][h] for h in range(2)]
    flow = []
    for f in range(2):
        once = [
            mask[h]
            * (
                (rings[f][0][h] + rings[f][1][h])
                + (rings[f][2][h] + rings[f][3][h])
                - unit[h] * flat[f][h]
            )
            for h in range(2)
        ]
        ring = around(once)
        sign = 1.0 - 2.0 * f
        total_flow = []
        for h in range(2):
            if f == 0:
                slope = rings[2][1][h] - rings[2][0][h] + weights[h, 6] * flat[2][h]
            else:
                slope = rings[2][3][h] - rings[2][2][h] + weights[h, 7] * flat[2][h]
            smooth = (
                weights[h, 8] * rings[f][0][h]
                + weights[h, 9] * rings[f][1][h]
                + (weights[h, 10] * rings[f][2][h] + weights[h, 11] * rings[f][3][h])
                - weights[h, 12] * flat[f][h]
            )
            twice = (ring[0][h] + ring[1][h]) + (ring[2][h] + ring[3][h]) - unit[h] * once[h]
            total_flow.append(
                mask[h]
                * (
                    flat[f][h]
                    + sign * buf2[h, 3] * flat[1 - f][h]
                    - (0.5 * pressure_coef) * slope
                    + smooth
                    - biharmonic_coef * twice
                )
            )
        flow.append(total_flow)
    flow_u, flow_v = flow
    before, after = left(flow_v), right(flow_v)
    vectors = [
        [
            mask[h]
            * (
                surface_coef * buf2[h, 2]
                - (0.5 * divergence_coef)
                * ((down(flow_u[h]) - up(flow_u[h])) + (after[h] - before[h]))
            )
            * inverse[h]
            for h in range(2)
        ]
    ]
    for _ in range(ITERS):
        ring = around(vectors[-1])
        vectors.append(
            [
                (
                    (face[h][0] * ring[0][h] + face[h][1] * ring[1][h])
                    + (face[h][2] * ring[2][h] + face[h][3] * ring[3][h])
                )
                * inverse[h]
                for h in range(2)
            ]
        )
    inside = slice(HALO, HALO + half)
    basis = [[pair[h][inside] for h in range(2)] for pair in vectors]
    scale = [scaling[h][inside] for h in range(2)]

    def dot(a, b):
        both = scale[0] * a[0] * b[0] + scale[1] * a[1] * b[1]
        return jnp.sum(both, axis=0, keepdims=True)

    moments = 2 * ITERS - 1
    difference = [
        [basis[k][h] - basis[k + 1][h] for h in range(2)] for k in range(ITERS)
    ]
    gathered[me] = jnp.zeros(gathered.shape[1:], jnp.float32)
    lines = [dot(basis[(k + 1) // 2], basis[k // 2]) for k in range(moments)]
    lines += [dot(basis[(k + 1) // 2], difference[k // 2]) for k in range(moments)]
    for k, line in enumerate(lines):
        gathered[me, k : k + 1, :] = line

    def gram(k):
        peer = lax.rem(me + k, peers)
        return pltpu.make_async_remote_copy(
            src_ref=gathered.at[me],
            dst_ref=gathered.at[me],
            send_sem=gram_send.at[k],
            recv_sem=gram_recv.at[me],
            device_id=(group, peer // 2, lax.rem(peer, 2)),
            device_id_type=MESH,
        )

    def gram_from(k):
        peer = lax.rem(me + k, peers)
        return pltpu.make_async_remote_copy(
            src_ref=gathered.at[peer],
            dst_ref=gathered.at[peer],
            send_sem=gram_send.at[k],
            recv_sem=gram_recv.at[peer],
            device_id=(group, peer // 2, lax.rem(peer, 2)),
            device_id_type=MESH,
        )

    def gram_start(k, _):
        gram(k).start()
        return 0

    def gram_wait(k, _):
        gram_from(k).wait_recv()
        return 0

    def gram_sent(k, _):
        gram(k).wait_send()
        return 0

    lax.fori_loop(1, peers, gram_start, 0)
    for h in range(2):
        for j in range(ITERS + 1):
            krylov[h, j] = basis[j][h]
        krylov[h, ITERS + 1] = scale[h]

    for h in range(2):
        for i in range(4):
            total[h, i] = jnp.zeros((span, columns), jnp.float32)

    def level(l, _):
        thickness = thick_ref[l]
        fields = []
        rings = []
        for f in range(3):
            pair = [buf[h, f, l] * weights[h, 0] for h in range(2)]
            fields.append(pair)
            rings.append(around(pair))
        u, v, t = fields
        viscous_part = []
        for f in range(3):
            viscous_part.append(
                [
                    weights[h, 8] * rings[f][0][h]
                    + weights[h, 9] * rings[f][1][h]
                    + (weights[h, 10] * rings[f][2][h] + weights[h, 11] * rings[f][3][h])
                    - weights[h, 12] * fields[f][h]
                    for h in range(2)
                ]
            )
        hyper = []
        for f in range(2):
            once = [
                weights[h, 0]
                * (
                    (rings[f][0][h] + rings[f][1][h])
                    + (rings[f][2][h] + rings[f][3][h])
                    - weights[h, 1] * fields[f][h]
                )
                for h in range(2)
            ]
            ring = around(once)
            hyper.append(
                [
                    (ring[0][h] + ring[1][h]) + (ring[2][h] + ring[3][h]) - weights[h, 1] * once[h]
                    for h in range(2)
                ]
            )
        tu, td, tl, tr = rings[2]
        uu, ud, _, _ = rings[0]
        _, _, vl, vr = rings[1]
        for h in range(2):
            m = weights[h, 0]
            slope_row = thickness * (td[h] - tu[h] + weights[h, 6] * t[h])
            slope_column = thickness * (tr[h] - tl[h] + weights[h, 7] * t[h])
            sum_row = total[h, 2] + slope_row
            sum_column = total[h, 3] + slope_column
            total[h, 2] = sum_row
            total[h, 3] = sum_column
            grad_row = sum_row - 0.5 * slope_row
            grad_column = sum_column - 0.5 * slope_column
            spread = (
                weights[h, 3] * ((u[h] + ud[h]) * (t[h] + td[h]))
                - weights[h, 2] * ((u[h] + uu[h]) * (t[h] + tu[h]))
                + (
                    weights[h, 5] * ((v[h] + vr[h]) * (t[h] + tr[h]))
                    - weights[h, 4] * ((v[h] + vl[h]) * (t[h] + tl[h]))
                )
            )
            spin = buf2[h, 3]
            u_next = m * (
                u[h]
                + spin * v[h]
                - (0.5 * pressure_coef) * grad_row
                + viscous_part[0][h]
                - biharmonic_coef * hyper[0][h]
            )
            v_next = m * (
                v[h]
                - spin * u[h]
                - (0.5 * pressure_coef) * grad_column
                + viscous_part[1][h]
                - biharmonic_coef * hyper[1][h]
            )
            t_next = m * (t[h] - (0.25 * advection_coef) * spread + viscous_part[2][h])
            res[h, 0, l] = u_next[HALO : HALO + half]
            res[h, 1, l] = v_next[HALO : HALO + half]
            res[h, 2, l] = t_next[HALO : HALO + half]
        return 0

    mine = pl.ds(pl.multiple_of(half * core, 8), half)

    def outs(k):
        part = pl.ds(k * per, per)
        local = [
            pltpu.make_async_copy(
                res.at[core, f, part], ref.at[part, mine, :], out_sem.at[f, k]
            )
            for f, ref in enumerate((ou_ref, ov_ref, ot_ref))
        ]
        remote = [
            pltpu.make_async_remote_copy(
                src_ref=res.at[other, f, part],
                dst_ref=ref.at[part, mine, :],
                send_sem=back_send.at[f, k],
                recv_sem=back_recv.at[f, k],
                device_id=(group, gx, other),
                device_id_type=MESH,
            )
            for f, ref in enumerate((ou_ref, ov_ref, ot_ref))
        ]
        return remote + local

    def chunk(k, _):
        arrive(k)
        lax.fori_loop(k * per, (k + 1) * per, level, 0)
        for copy in outs(k):
            copy.start()
        return 0

    lax.fori_loop(0, CHUNKS, chunk, 0)

    lax.fori_loop(1, peers, gram_wait, 0)

    summed = lax.fori_loop(
        0, peers, lambda k, acc: acc + gathered[k], jnp.zeros(gathered.shape[1:], jnp.float32)
    )
    sums = jnp.sum(summed, axis=1, keepdims=True)
    mass = [sums[k : k + 1] for k in range(moments)]
    stiff = [sums[moments + k : moments + k + 1] for k in range(moments)]

    def quadratic(coefs, table):
        value = None
        for i, a in enumerate(coefs):
            for j, b in enumerate(coefs):
                term = a * b * table[i + j]
                value = term if value is None else value + term
        return value

    one = jnp.ones((1, 1), jnp.float32)
    zero = jnp.zeros((1, 1), jnp.float32)
    remains = [one]
    heading = [one]
    guess = [zero] * ITERS
    rho = mass[0]
    for iteration in range(ITERS):
        step = rho / quadratic(heading, stiff)
        for j, c in enumerate(heading):
            guess[j] = guess[j] + step * c
        moved = remains + [zero]
        for j, c in enumerate(heading):
            moved[j] = moved[j] - step * c
            moved[j + 1] = moved[j + 1] + step * c
        remains = moved
        if iteration + 1 < ITERS:
            rho_new = quadratic(remains, mass)
            ratio = rho_new / rho
            heading = [
                remains[j] + ratio * heading[j] if j < len(heading) else remains[j]
                for j in range(len(remains))
            ]
            rho = rho_new

    for h in range(2):
        x = guess[0] * krylov[h, 0]
        for j in range(1, ITERS):
            x = x + guess[j] * krylov[h, j]
        r = remains[0] * krylov[h, 0]
        for j in range(1, ITERS + 1):
            r = r + remains[j] * krylov[h, j]
        res2[h, 0] = x
        res2[h, 1] = krylov[h, ITERS + 1] * r

    def flat_outs():
        k = CHUNKS
        local = [
            pltpu.make_async_copy(res2.at[core, f], ref.at[mine, :], out_sem.at[f, k])
            for f, ref in enumerate((ox_ref, or_ref))
        ]
        remote = [
            pltpu.make_async_remote_copy(
                src_ref=res2.at[other, f],
                dst_ref=ref.at[mine, :],
                send_sem=back_send.at[f, k],
                recv_sem=back_recv.at[f, k],
                device_id=(group, gx, other),
                device_id_type=MESH,
            )
            for f, ref in enumerate((ox_ref, or_ref))
        ]
        return remote + local

    for copy in flat_outs():
        copy.start()
    lax.fori_loop(1, peers, gram_sent, 0)
    sent(None)
    for k in range(CHUNKS):
        sent(k)
        for copy in outs(k):
            copy.wait()
    for copy in flat_outs():
        copy.wait()


def deliver(*refs):
    sources, targets, held = refs[:5], refs[5:10], refs[10:15]
    into_sem, out_sem = refs[15:]

    def cut(ref, k):
        size = ref.shape[0] // CHUNKS
        return ref.at[pl.ds(k * size, size)]

    pieces = [(i, k) for k in range(CHUNKS) for i in range(5)]
    into = [
        pltpu.make_async_copy(cut(sources[i], k), cut(held[i], k), into_sem.at[i, k])
        for i, k in pieces
    ]
    out = [
        pltpu.make_async_copy(cut(held[i], k), cut(targets[i], k), out_sem.at[i, k])
        for i, k in pieces
    ]
    for copy in into:
        copy.start()
    for first, second in zip(into, out):
        first.wait()
        second.start()
    for copy in out:
        copy.wait()


def per_device(count, *args):
    u, v, t, spin, thick, visc, depth, sea, wet = args
    levels, rows, columns = u.shape
    half = rows // 2
    span = half + 2 * HALO
    assert rows == TS and columns == 2 * TS
    peers = 2 * count
    f32 = jnp.float32
    anywhere = pl.BlockSpec(memory_space=pl.ANY)
    vmem = pl.BlockSpec(memory_space=pltpu.VMEM)
    smem = pl.BlockSpec(memory_space=pltpu.SMEM)
    dma = pltpu.SemaphoreType.DMA
    fields = pl.pallas_call(
        functools.partial(kernel, count),
        out_shape=[jax.ShapeDtypeStruct(u.shape, f32)] * 3
        + [jax.ShapeDtypeStruct(sea.shape, f32)] * 2,
        in_specs=[anywhere, anywhere, anywhere, vmem, smem, anywhere, anywhere, anywhere, smem],
        out_specs=[anywhere] * 5,
        scratch_shapes=[
            pltpu.VMEM((3, levels, rows, columns), f32),
            pltpu.VMEM((4, rows, columns), f32),
            pltpu.VMEM((2, 3, levels, span, columns), f32),
            pltpu.VMEM((2, 7, span, columns), f32),
            pltpu.VMEM((2, 3, levels, half, columns), f32),
            pltpu.VMEM((2, 2, half, columns), f32),
            pltpu.VMEM((2, 13, span, columns), f32),
            pltpu.VMEM((2, 4, span, columns), f32),
            pltpu.VMEM((2, ITERS + 2, half, columns), f32),
            pltpu.VMEM((peers, 16, columns), f32),
            dma((3,)),
            dma((3, CHUNKS + 1)),
            dma((7, CHUNKS + 1)),
            dma((7, CHUNKS + 1)),
            dma((2, 7, CHUNKS + 1)),
            dma((2, 7, CHUNKS + 1)),
            dma((3, CHUNKS + 1)),
            dma((3, CHUNKS + 1)),
            dma((3, CHUNKS + 1)),
            dma((peers,)),
            dma((peers,)),
        ],
        compiler_params=pltpu.CompilerParams(
            collective_id=0, has_side_effects=True, vmem_limit_bytes=VMEM_BYTES
        ),
    )(u, v, t, spin.reshape(1, rows), thick, visc, depth, sea, wet.T)
    return pl.pallas_call(
        deliver,
        out_shape=[jax.ShapeDtypeStruct(a.shape, f32) for a in fields],
        in_specs=[anywhere] * 5,
        out_specs=[anywhere] * 5,
        scratch_shapes=[pltpu.VMEM(a.shape, f32) for a in fields]
        + [dma((5, CHUNKS)), dma((5, CHUNKS))],
        compiler_params=pltpu.CompilerParams(vmem_limit_bytes=VMEM_BYTES),
    )(*fields)


def solution(mesh):
    cells = P(None, ("group", "gx"), "gy")
    flat = P(("group", "gx"), "gy")
    assert mesh.shape["gy"] == 2
    return jax.shard_map(
        functools.partial(per_device, mesh.shape["gx"]),
        mesh=mesh,
        in_specs=(cells, cells, cells, P("gx"), P(), P("gx", "gy"), P("gx", "gy"), flat, P()),
        out_specs=(cells, cells, cells, flat, flat),
        check_vma=False,
    )
```
